1024 devices in a mesh: slab: 64 (over x, y), head: 16 (over z, core).
Axes of the slice: x: 8, y: 8, z: 8, core: 2. Of those that a mesh axis runs over, the one named last changes fastest.
Arguments:
- queries: bfloat16 [131072, 1024], P(('slab', 'head')), may hold values from -8 to 8
- keys: bfloat16 [131072, 1024], P(('slab', 'head')), may hold values from -8 to 8
- values: bfloat16 [131072, 1024], P(('slab', 'head')), may hold values from -6 to 6
- out_grad: bfloat16 [131072, 1024], P(('slab', 'head')), may hold values from -6 to 6
- links: int32 [64, 40, 2], replicated, may hold values from -1 to 79, as said below
- wanted: int32 [64, 64], replicated, may hold values from 0 to 15
Outputs:
- attended: bfloat16 [131072, 1024], P(('slab', 'head'))
- query_grad: bfloat16 [131072, 1024], P(('slab', 'head'))
- key_grad: bfloat16 [131072, 1024], P(('slab', 'head'))
- value_grad: bfloat16 [131072, 1024], P(('slab', 'head'))
The draws below stay inside these ranges and needn't reach their ends.
Inputs may be any that keep to these rules, and one draw needn't show every extreme that they name: links[t, j] = (query block, key slot). The first 16 links of every slab are (b, b) for b = 0 to 15; the used links come next, then unused ones stored as (-1, 0). Key slot 16 + u never names the slab itself. In every draw some slab uses all 40 links, some slab leaves links unused, and some slab is named by every other slab.
All inputs are finite; a program needn't handle non-finite values.
Results may differ from the reference program's by a relative error of at most 0.011.
Values may be sent and summed in bfloat16 or wider, within the bound.
No kernel may reach another device: no remote copies, remote signals or barrier semaphores. Data moves between devices by JAX's collectives and lax.ppermute only.
A program may use at most 64 MiB of HBM per device.

```python
import math
import jax
import jax.numpy as jnp
from jax import lax

D = 1024
HEADS = 16
HD = 64
BLK = 128
NB = 16
LINKS = 40
NODES = 131072
N_SLAB = 64


def draw_queries(key, part):
    key = jax.random.fold_in(key, 1)
    return jnp.clip(jax.random.normal(key, (NODES, D), jnp.float32), -6.0, 6.0).astype(jnp.bfloat16)


def draw_keys(key, part):
    key = jax.random.fold_in(key, 3)
    return jnp.clip(jax.random.normal(key, (NODES, D), jnp.float32), -6.0, 6.0).astype(jnp.bfloat16)


def draw_links(key, part):
    key = jax.random.fold_in(key, 5)
    subkeys = jax.random.split(key, 8)
    slab_ids = jnp.arange(N_SLAB, dtype=jnp.int32)[:, None]
    link_pos = jnp.arange(LINKS, dtype=jnp.int32)[None, :]
    busiest = jax.random.randint(subkeys[0], (), 0, N_SLAB)
    popular = jax.random.randint(subkeys[1], (), 0, N_SLAB)
    lightest = (busiest + 1) % N_SLAB
    heavy_slab = (jax.random.randint(subkeys[2], (N_SLAB, 1), 0, 8) == 0) & (slab_ids != lightest) | (slab_ids == busiest)
    live_count = jnp.where(heavy_slab, LINKS, jax.random.randint(subkeys[3], (N_SLAB, 1), NB + 1, NB * 3 // 2 + 1))
    extra_pos = link_pos - NB
    peer_slab = (slab_ids + 1 + jax.random.randint(subkeys[4], (N_SLAB, LINKS), 0, N_SLAB - 1)) % N_SLAB
    remote = jax.random.randint(subkeys[5], (N_SLAB, LINKS), 0, 2) == 1
    popular_peer = jnp.where(popular == N_SLAB - 1, 0, N_SLAB - 1)
    first_peer = jnp.where(slab_ids == popular, popular_peer, popular)
    peer_slab = jnp.where(extra_pos == 0, first_peer, peer_slab)
    remote = remote | (extra_pos == 0)
    local_key = jax.random.randint(subkeys[6], (N_SLAB, LINKS), 0, NB)
    query_blk = jax.random.randint(subkeys[7], (N_SLAB, LINKS), 0, NB)
    key_slot = jnp.where(remote, NB + peer_slab, local_key)
    own_link = link_pos < NB
    query_blk = jnp.where(own_link, link_pos, query_blk)
    key_slot = jnp.where(own_link, link_pos, key_slot)
    is_live = link_pos < live_count
    query_blk = jnp.where(is_live, query_blk, -1)
    key_slot = jnp.where(is_live, key_slot, 0)
    return jnp.stack([query_blk, key_slot], -1).astype(jnp.int32)


def set_ends(result, own_key, smallest, top_value):
    longest = result.shape.index(max(result.shape))
    spots = []
    for shift in (0, 1):
        where = [jax.random.randint(jax.random.fold_in(own_key, axis), (), 0, length) for axis, length in enumerate(result.shape)]
        where[longest] = (where[longest] + shift) % result.shape[longest]
        spots.append(tuple(where))
    return result.at[spots[0]].set(smallest).at[spots[1]].set(top_value)


def block_scale(key, extent, cuts, low, high):
    factor_of = 1.0
    for dim, blocks in cuts:
        heights = jax.random.uniform(jax.random.fold_in(jax.random.fold_in(key, 6), dim), (blocks,), jnp.float32, low / len(cuts), high / len(cuts))
        factor_of = factor_of * jnp.repeat(jnp.exp(heights), extent[dim] // blocks).reshape((-1,) + (1,) * (len(extent) - 1 - dim))
    return factor_of


def noise(rng, dims, deviation, reach, pieces=(), held_as=jnp.bfloat16):
    drawn = deviation * jax.random.normal(rng, dims, jnp.float32)
    if pieces:
        drawn = drawn * block_scale(rng, dims, pieces, -0.22, 0.18)
    return jnp.clip(drawn, -reach, reach).astype(held_as)


def setup_inputs(seed: int = 0) -> dict:
    splits = jax.random.split(jax.random.key(seed), 7)
    queries = draw_queries(jax.random.fold_in(splits[6], 71), 0)
    keys = draw_keys(jax.random.fold_in(splits[6], 71), 0)
    values = noise(splits[2], (NODES, D), 1.0, 6.0, ((0, 1024),))
    out_grad = noise(splits[3], (NODES, D), 1.0, 6.0, ((0, 1024),))
    links = draw_links(jax.random.fold_in(splits[6], 71), 0)
    wanted = set_ends(jax.random.randint(splits[5], (N_SLAB, N_SLAB), 0, NB), jax.random.fold_in(splits[5], 1), 0, NB - 1).astype(jnp.int32)
    return dict(queries=queries, keys=keys, values=values, out_grad=out_grad, links=links, wanted=wanted)


highest = lax.Precision.HIGHEST

def slab_pass(q_own, k_table, v_table, g_own, link_list):
    score_scale = 1.0 / math.sqrt(HD)
    queried = link_list[:, 0]
    key_slot = link_list[:, 1]
    is_valid = queried >= 0
    query_safe = jnp.maximum(queried, 0)
    block_ids = jnp.arange(NB, dtype=jnp.int32)
    slot_ids = jnp.arange(NB + N_SLAB, dtype=jnp.int32)
    query_hit = (queried[:, None] == block_ids[None, :]).astype(jnp.float32)
    slot_hit = ((key_slot[:, None] == slot_ids[None, :]) & is_valid[:, None]).astype(jnp.float32)
    q_sel = jnp.take(q_own, query_safe, 0).astype(jnp.float32)
    g_sel = jnp.take(g_own, query_safe, 0).astype(jnp.float32)
    k_sel = jnp.take(k_table, key_slot, 0).astype(jnp.float32)
    v_sel = jnp.take(v_table, key_slot, 0).astype(jnp.float32)
    scores = jnp.einsum('lqhd,lkhd->lhqk', q_sel, k_sel) * score_scale
    row_max = scores.max(-1)
    row_top = lax.optimization_barrier(jnp.max(jnp.where(query_hit[:, :, None, None] > 0, row_max[:, None], -jnp.inf), 0))
    raised = jnp.where(is_valid[:, None, None, None], jnp.exp(scores - jnp.take(row_top, query_safe, 0)[..., None]), 0.0)
    row_total = jnp.einsum('ln,lhq->nhq', query_hit, raised.sum(-1), precision=highest)
    prob_bf = (raised / jnp.take(row_total, query_safe, 0)[..., None]).astype(jnp.bfloat16)
    prob_full = lax.optimization_barrier(prob_bf).astype(jnp.float32)
    links_here = link_list.shape[0]
    mixed_part = jnp.einsum('lhqk,lkhd->lqhd', prob_full, v_sel).reshape(links_here, -1)
    attended = jnp.einsum('ln,lx->nx', query_hit, mixed_part, precision=highest)
    attended = attended.reshape(NB, BLK, HEADS, HD).astype(jnp.bfloat16)
    delta_rows = jnp.transpose(lax.optimization_barrier(jnp.sum(g_own.astype(jnp.float32) * attended.astype(jnp.float32), -1)), (0, 2, 1))
    d_prob = jnp.einsum('lqhd,lkhd->lhqk', g_sel, v_sel)
    d_score = (prob_full * (d_prob - jnp.take(delta_rows, query_safe, 0)[..., None]) * score_scale).astype(jnp.bfloat16)
    d_score = lax.optimization_barrier(d_score).astype(jnp.float32)
    dq_part = jnp.einsum('lhqk,lkhd->lqhd', d_score, k_sel).reshape(links_here, -1)
    query_grad = jnp.einsum('ln,lx->nx', query_hit, dq_part, precision=highest)
    query_grad = query_grad.reshape(NB, BLK, HEADS, HD).astype(jnp.bfloat16)
    dk_part = jnp.einsum('lhqk,lqhd->lkhd', d_score, q_sel).reshape(links_here, -1)
    dv_part = jnp.einsum('lhqk,lqhd->lkhd', prob_full, g_sel).reshape(links_here, -1)
    key_term = jnp.einsum('ls,lx->sx', slot_hit, dk_part, precision=highest).reshape(NB + N_SLAB, BLK, HEADS, HD)
    value_term = jnp.einsum('ls,lx->sx', slot_hit, dv_part, precision=highest).reshape(NB + N_SLAB, BLK, HEADS, HD)
    return (attended, query_grad, key_term, value_term)

def reference(queries, keys, values, out_grad, links, wanted):
    full_shape = (N_SLAB, NB, BLK, HEADS, HD)
    q_blk = queries.reshape(full_shape)
    k_blk = keys.reshape(full_shape)
    v_blk = values.reshape(full_shape)
    g_blk = out_grad.reshape(full_shape)
    slab_ids = jnp.arange(N_SLAB, dtype=jnp.int32)

    def slab_step(running, slab_id):
        acc_keys, acc_values = running
        wanted_row = wanted[slab_id].astype(jnp.int32)
        k_table = jnp.concatenate([k_blk[slab_id], k_blk[slab_ids, wanted_row]], 0)
        v_table = jnp.concatenate([v_blk[slab_id], v_blk[slab_ids, wanted_row]], 0)
        attended, query_grad, key_term, value_term = slab_pass(q_blk[slab_id], k_table, v_table, g_blk[slab_id], links[slab_id])
        far_keys = lax.optimization_barrier(key_term[NB:].astype(jnp.bfloat16)).astype(jnp.float32)
        far_values = lax.optimization_barrier(value_term[NB:].astype(jnp.bfloat16)).astype(jnp.float32)
        acc_keys = acc_keys.at[slab_id].add(key_term[:NB]).at[slab_ids, wanted_row].add(far_keys)
        acc_values = acc_values.at[slab_id].add(value_term[:NB]).at[slab_ids, wanted_row].add(far_values)
        return ((acc_keys, acc_values), (attended, query_grad))
    zeros_full = jnp.zeros(full_shape, jnp.float32)
    (acc_keys, acc_values), (attended, query_grad) = lax.scan(slab_step, (zeros_full, zeros_full), slab_ids)
    whole = (NODES, D)
    return (attended.reshape(whole), query_grad.reshape(whole), acc_keys.astype(jnp.bfloat16).reshape(whole), acc_values.astype(jnp.bfloat16).reshape(whole))
```

```python
import math

import jax
import jax.numpy as jnp
from jax import lax
from jax.experimental import pallas as pl
from jax.experimental.pallas import tpu as pltpu
from jax.sharding import PartitionSpec as P

HD = 64
BLK = 128
PAIR = 2 * HD
UNROLL = 8
LIMIT = 48 * 1024 * 1024

VMEM = pl.BlockSpec(memory_space=pltpu.VMEM)
SMEM = pl.BlockSpec(memory_space=pltpu.SMEM)


def cost(flops, moved, exps=0):
    return pl.CostEstimate(flops=flops, bytes_accessed=moved, transcendentals=exps)


def pack_kernel(q_ref, k_ref, v_ref, g_ref, out_ref):
    for first_ref, second_ref, row in ((k_ref, v_ref, 0), (q_ref, g_ref, BLK)):
        for h in range(out_ref.shape[0]):
            cols = slice(h * HD, (h + 1) * HD)
            out_ref[h, row : row + BLK, :] = jnp.concatenate(
                [first_ref[:, cols], second_ref[:, cols]], axis=1
            )


def unpack_kernel(in_ref, o_ref, dq_ref, dk_ref, dv_ref):
    for first_ref, second_ref, row in ((dq_ref, o_ref, 0), (dk_ref, dv_ref, BLK)):
        for h in range(0, in_ref.shape[0], 2):
            even = in_ref[h, row : row + BLK, :]
            odd = in_ref[h + 1, row : row + BLK, :]
            cols = slice(h * HD, (h + 2) * HD)
            first_ref[:, cols] = jnp.concatenate([even[:, :HD], odd[:, :HD]], axis=1)
            second_ref[:, cols] = jnp.concatenate([even[:, HD:], odd[:, HD:]], axis=1)


def attend_kernel(
    links_ref,
    near_ref,
    far_ref,
    odq_ref,
    home_ref,
    far_out_ref,
    table,
    masked,
    s_buf,
    d_buf,
    top,
    total,
    delta,
    acc,
    dkv,
):
    blocks, slots = near_ref.shape[0], table.shape[0]
    link_count = links_ref.shape[0]
    score_scale = 1.0 / math.sqrt(HD)
    exp_scale = score_scale * math.log2(math.e)
    left = lax.broadcasted_iota(jnp.int32, (BLK, PAIR), 1) < HD

    for b in range(blocks):
        table[b] = near_ref[b, :BLK, :]
        qg = near_ref[b, BLK:, :]
        masked[b, :BLK, :] = jnp.where(left, qg, jnp.zeros_like(qg))
        masked[b, BLK:, :] = jnp.where(left, jnp.zeros_like(qg), qg)
    table[blocks:] = far_ref[...]
    top[...] = jnp.full_like(top, -3e38)
    total[...] = jnp.zeros_like(total)
    delta[...] = jnp.zeros_like(delta)
    acc[...] = jnp.zeros_like(acc)
    dkv[...] = jnp.zeros_like(dkv)

    def each_link(step):
        def group(i, _):
            for r in range(UNROLL):
                j = i * UNROLL + r
                queried = links_ref[j, 0]
                step(j, jnp.maximum(queried, 0), links_ref[j, 1], queried >= 0)
            return 0

        lax.fori_loop(0, link_count // UNROLL, group, 0)

    def score_step(j, b, s, valid):
        both = lax.dot_general(
            table[s], masked[b], (((1,), (1,)), ((), ())), preferred_element_type=jnp.float32
        )
        s_buf[j] = both[:, :BLK]
        d_buf[j] = both[:, BLK:]
        largest = jnp.max(both[:, :BLK], axis=0, keepdims=True)
        top[b] = jnp.maximum(top[b], jnp.where(valid, largest, -3e38))

    def sum_step(j, b, s, valid):
        shift = top[b] + jnp.where(valid, 0.0, 1e30)
        raised = jnp.exp2((s_buf[j] - shift) * exp_scale)
        s_buf[j] = raised
        total[b] = total[b] + jnp.sum(raised, axis=0, keepdims=True)
        delta[b] = delta[b] + jnp.sum(raised * d_buf[j], axis=0, keepdims=True)

    def grad_step(j, b, s, valid):
        prob = (s_buf[j] * total[b]).astype(jnp.bfloat16)
        dscore = (prob.astype(jnp.float32) * (d_buf[j] - delta[b]) * score_scale).astype(
            jnp.bfloat16
        )
        turned = lax.dot_general(
            table[s],
            jnp.concatenate([prob, dscore], axis=1),
            (((0,), (0,)), ((), ())),
            preferred_element_type=jnp.float32,
        )
        acc[b, :HD, :] += turned[:HD, BLK:]
        acc[b, HD:, :] += turned[HD:, :BLK]
        terms = jnp.dot(
            jnp.concatenate([dscore, prob], axis=0),
            near_ref[b, BLK:, :],
            preferred_element_type=jnp.float32,
        )
        dkv[s] += jnp.where(left, terms[:BLK], terms[BLK:])

    each_link(score_step)
    each_link(sum_step)
    inverse = 1.0 / total[...]
    delta[...] = delta[...] * inverse
    total[...] = inverse
    each_link(grad_step)

    for b in range(blocks):
        odq_ref[b] = acc[b].T.astype(jnp.bfloat16)
    home_ref[...] = dkv[:blocks]
    far_out_ref[...] = dkv[blocks:].astype(jnp.bfloat16)


def combine_kernel(given_ref, home_ref, returned_ref, odq_ref, out_ref, acc):
    acc[...] = home_ref[...]

    def group(i, _):
        for r in range(UNROLL):
            t = i * UNROLL + r
            acc[given_ref[t]] += returned_ref[t].astype(jnp.float32)
        return 0

    lax.fori_loop(0, returned_ref.shape[0] // UNROLL, group, 0)
    out_ref[:, :BLK, :] = odq_ref[...]
    out_ref[:, BLK:, :] = acc[...].astype(jnp.bfloat16)


def body(queries, keys, values, out_grad, links, wanted):
    slabs = lax.axis_size("slab")
    blocks = lax.axis_size("head")
    slab_index = lax.axis_index("slab")
    link_count = links.shape[1]
    slots = blocks + slabs
    bf, f32 = jnp.bfloat16, jnp.float32
    params = pltpu.CompilerParams(vmem_limit_bytes=LIMIT)
    tile = (BLK, PAIR)
    tile_bytes = 2 * BLK * PAIR

    packed = pl.pallas_call(
        pack_kernel,
        out_shape=jax.ShapeDtypeStruct((blocks, 2 * BLK, PAIR), bf),
        in_specs=[VMEM] * 4,
        out_specs=VMEM,
        compiler_params=params,
        cost_estimate=cost(0, 4 * blocks * tile_bytes),
        name="pack",
    )(queries, keys, values, out_grad)
    near = lax.all_to_all(packed, "head", split_axis=0, concat_axis=0, tiled=True)

    own_links = lax.dynamic_index_in_dim(links, slab_index, 0, keepdims=False)
    given = lax.dynamic_index_in_dim(wanted, slab_index, 1, keepdims=False)
    outgoing = jnp.take(near[:, :BLK, :], given, 0)
    far = lax.all_to_all(outgoing, "slab", split_axis=0, concat_axis=0, tiled=True)

    odq, home, far_out = pl.pallas_call(
        attend_kernel,
        out_shape=(
            jax.ShapeDtypeStruct((blocks, *tile), bf),
            jax.ShapeDtypeStruct((blocks, *tile), f32),
            jax.ShapeDtypeStruct((slabs, *tile), bf),
        ),
        in_specs=[SMEM, VMEM, VMEM],
        out_specs=(VMEM, VMEM, VMEM),
        scratch_shapes=[
            pltpu.VMEM((slots, *tile), bf),
            pltpu.VMEM((blocks, 2 * BLK, PAIR), bf),
            pltpu.VMEM((link_count, BLK, BLK), f32),
            pltpu.VMEM((link_count, BLK, BLK), f32),
            pltpu.VMEM((blocks, 1, BLK), f32),
            pltpu.VMEM((blocks, 1, BLK), f32),
            pltpu.VMEM((blocks, 1, BLK), f32),
            pltpu.VMEM((blocks, PAIR, BLK), f32),
            pltpu.VMEM((slots, *tile), f32),
        ],
        compiler_params=params,
        cost_estimate=cost(
            link_count * 6 * BLK * BLK * PAIR * 2,
            (2 * slabs + 4 * blocks) * tile_bytes,
            link_count * BLK * BLK,
        ),
        name="attend",
    )(own_links, near, far)

    returned = lax.all_to_all(far_out, "slab", split_axis=0, concat_axis=0, tiled=True)
    results = pl.pallas_call(
        combine_kernel,
        out_shape=jax.ShapeDtypeStruct((blocks, 2 * BLK, PAIR), bf),
        in_specs=[SMEM, VMEM, VMEM, VMEM],
        out_specs=VMEM,
        scratch_shapes=[pltpu.VMEM((blocks, *tile), f32)],
        compiler_params=params,
        cost_estimate=cost(0, (slabs + 4 * blocks) * tile_bytes),
        name="combine",
    )(given, home, returned, odq)
    mine = lax.all_to_all(results, "head", split_axis=0, concat_axis=0, tiled=True)
    return pl.pallas_call(
        unpack_kernel,
        out_shape=tuple(jax.ShapeDtypeStruct(queries.shape, bf) for _ in range(4)),
        in_specs=[VMEM],
        out_specs=(VMEM,) * 4,
        compiler_params=params,
        cost_estimate=cost(0, 4 * blocks * tile_bytes),
        name="unpack",
    )(mine)


def solution(mesh):
    rows = P(("slab", "head"), None)
    return jax.shard_map(
        body,
        mesh=mesh,
        in_specs=(rows, rows, rows, rows, P(), P()),
        out_specs=(rows,) * 4,
        check_vma=False,
    )
```

```python
import functools
import math

import jax
import jax.numpy as jnp
from jax import lax
from jax.experimental import pallas as pl
from jax.experimental.pallas import tpu as pltpu
from jax.sharding import PartitionSpec as P

HD = 64
BLK = 128
PAIR = 2 * HD
UNROLL = 8
LIMIT = 48 * 1024 * 1024

VMEM = pl.BlockSpec(memory_space=pltpu.VMEM)
SMEM = pl.BlockSpec(memory_space=pltpu.SMEM)


def cost(flops, moved, exps=0):
    return pl.CostEstimate(flops=flops, bytes_accessed=moved, transcendentals=exps)


def pack_kernel(q_ref, k_ref, v_ref, g_ref, out_ref):
    for first_ref, second_ref, row in ((k_ref, v_ref, 0), (q_ref, g_ref, BLK)):
        for h in range(out_ref.shape[0]):
            cols = slice(h * HD, (h + 1) * HD)
            out_ref[h, row : row + BLK, :] = jnp.concatenate(
                [first_ref[:, cols], second_ref[:, cols]], axis=1
            )


def unpack_kernel(in_ref, o_ref, dq_ref, dk_ref, dv_ref):
    for first_ref, second_ref, row in ((dq_ref, o_ref, 0), (dk_ref, dv_ref, BLK)):
        for h in range(0, in_ref.shape[0], 2):
            even = in_ref[h, row : row + BLK, :]
            odd = in_ref[h + 1, row : row + BLK, :]
            cols = slice(h * HD, (h + 2) * HD)
            first_ref[:, cols] = jnp.concatenate([even[:, :HD], odd[:, :HD]], axis=1)
            second_ref[:, cols] = jnp.concatenate([even[:, HD:], odd[:, HD:]], axis=1)


def each_piece(slabs, held):
    parts = BLK // slabs
    for c in range(held):
        for part in range(parts):
            yield c, slice(part * slabs, (part + 1) * slabs), pl.ds(
                part * held + c, slabs, stride=parts * held
            )


def spread_kernel(near_ref, out_ref, wide, *, slabs):
    for c, rows, piece_rows in each_piece(slabs, near_ref.shape[0]):
        wide[piece_rows, :] = near_ref[c, rows, :].astype(jnp.float32)
    out_ref[...] = wide[...].astype(jnp.bfloat16)


def gather_kernel(hot_ref, in_ref, out_ref, wide, *, slabs, blocks, extra):
    parts = BLK // slabs
    pieces = in_ref[...].reshape(slabs, parts, blocks, PAIR)
    source = jnp.concatenate(
        [pieces[:, part].reshape(slabs * blocks, PAIR) for part in range(parts)], axis=1
    )
    for t in range(0, slabs, UNROLL):
        picked = jnp.dot(
            hot_ref[t * extra : (t + UNROLL) * extra, :],
            source,
            preferred_element_type=jnp.float32,
        )
        for r in range(UNROLL):
            for part in range(parts):
                start = ((t + r) * parts + part) * extra
                wide[start : start + extra, :] = picked[
                    r * extra : (r + 1) * extra, part * PAIR : (part + 1) * PAIR
                ]
    out_ref[...] = wide[...].astype(jnp.bfloat16)


def reduce_kernel(hot_ref, in_ref, out_ref, wide, beside, *, slabs, blocks, extra):
    parts = BLK // slabs
    wide[...] = in_ref[...].astype(jnp.float32)
    for t in range(slabs):
        for part in range(parts):
            start = (t * parts + part) * extra
            beside[t * extra : (t + 1) * extra, part * PAIR : (part + 1) * PAIR] = wide[
                start : start + extra, :
            ]
    terms = beside[...].astype(jnp.bfloat16)
    for u in range(0, slabs, UNROLL):
        summed = jnp.dot(
            hot_ref[u * blocks : (u + UNROLL) * blocks, :],
            terms,
            preferred_element_type=jnp.float32,
        ).astype(jnp.bfloat16)
        for r in range(UNROLL):
            for part in range(parts):
                start = ((u + r) * parts + part) * blocks
                out_ref[start : start + blocks, :] = summed[
                    r * blocks : (r + 1) * blocks, part * PAIR : (part + 1) * PAIR
                ]


def attend_kernel(
    links_ref,
    near_ref,
    far_ref,
    odq_ref,
    home_ref,
    far_out_ref,
    table,
    masked,
    s_buf,
    d_buf,
    top,
    total,
    delta,
    acc,
    dkv,
    wide,
    *,
    slabs,
):
    blocks, slots = near_ref.shape[0], table.shape[0]
    link_count = links_ref.shape[0]
    score_scale = 1.0 / math.sqrt(HD)
    exp_scale = score_scale * math.log2(math.e)
    left = lax.broadcasted_iota(jnp.int32, (BLK, PAIR), 1) < HD

    wide[...] = far_ref[...].astype(jnp.float32)
    for p, rows, piece_rows in each_piece(slabs, slots - blocks):
        table[blocks + p, rows, :] = wide[piece_rows, :].astype(jnp.bfloat16)
    for b in range(blocks):
        table[b] = near_ref[b, :BLK, :]
        qg = near_ref[b, BLK:, :]
        masked[b, :BLK, :] = jnp.where(left, qg, jnp.zeros_like(qg))
        masked[b, BLK:, :] = jnp.where(left, jnp.zeros_like(qg), qg)
    top[...] = jnp.full_like(top, -3e38)
    total[...] = jnp.zeros_like(total)
    delta[...] = jnp.zeros_like(delta)
    acc[...] = jnp.zeros_like(acc)
    dkv[...] = jnp.zeros_like(dkv)

    def each_link(step):
        def group(i, _):
            for r in range(UNROLL):
                j = i * UNROLL + r
                queried = links_ref[j, 0]
                step(j, jnp.maximum(queried, 0), links_ref[j, 1], queried >= 0)
            return 0

        lax.fori_loop(0, link_count // UNROLL, group, 0)

    def score_step(j, b, s, valid):
        both = lax.dot_general(
            table[s], masked[b], (((1,), (1,)), ((), ())), preferred_element_type=jnp.float32
        )
        s_buf[j] = both[:, :BLK]
        d_buf[j] = both[:, BLK:]
        largest = jnp.max(both[:, :BLK], axis=0, keepdims=True)
        top[b] = jnp.maximum(top[b], jnp.where(valid, largest, -3e38))

    def sum_step(j, b, s, valid):
        shift = top[b] + jnp.where(valid, 0.0, 1e30)
        raised = jnp.exp2((s_buf[j] - shift) * exp_scale)
        s_buf[j] = raised
        total[b] = total[b] + jnp.sum(raised, axis=0, keepdims=True)
        delta[b] = delta[b] + jnp.sum(raised * d_buf[j], axis=0, keepdims=True)

    def grad_step(j, b, s, valid):
        prob = (s_buf[j] * total[b]).astype(jnp.bfloat16)
        dscore = (prob.astype(jnp.float32) * (d_buf[j] - delta[b]) * score_scale).astype(
            jnp.bfloat16
        )
        turned = lax.dot_general(
            table[s],
            jnp.concatenate([prob, dscore], axis=1),
            (((0,), (0,)), ((), ())),
            preferred_element_type=jnp.float32,
        )
        acc[b, :HD, :] += turned[:HD, BLK:]
        acc[b, HD:, :] += turned[HD:, :BLK]
        terms = jnp.dot(
            jnp.concatenate([dscore, prob], axis=0),
            near_ref[b, BLK:, :],
            preferred_element_type=jnp.float32,
        )
        dkv[s] += jnp.where(left, terms[:BLK], terms[BLK:])

    each_link(score_step)
    each_link(sum_step)
    inverse = 1.0 / total[...]
    delta[...] = delta[...] * inverse
    total[...] = inverse
    each_link(grad_step)

    for p, rows, piece_rows in each_piece(slabs, slots - blocks):
        wide[piece_rows, :] = dkv[blocks + p, rows, :]
    far_out_ref[...] = wide[...].astype(jnp.bfloat16)
    for b in range(blocks):
        odq_ref[b] = acc[b].T.astype(jnp.bfloat16)
    home_ref[...] = dkv[:blocks]


def combine_kernel(home_ref, returned_ref, odq_ref, out_ref, wide, *, slabs):
    wide[...] = returned_ref[...].astype(jnp.float32)
    for c, rows, piece_rows in each_piece(slabs, home_ref.shape[0]):
        start = BLK + rows.start
        out_ref[c, start : start + slabs, :] = (
            home_ref[c, rows, :] + wide[piece_rows, :]
        ).astype(jnp.bfloat16)
    out_ref[:, :BLK, :] = odq_ref[...]


def body(queries, keys, values, out_grad, links, wanted):
    slabs = lax.axis_size("slab")
    blocks = lax.axis_size("head")
    slab_index = lax.axis_index("slab")
    link_count = links.shape[1]
    extra = link_count - blocks
    parts = BLK // slabs
    bf, f32 = jnp.bfloat16, jnp.float32
    params = pltpu.CompilerParams(vmem_limit_bytes=LIMIT)
    tile = (BLK, PAIR)
    tile_bytes = 2 * BLK * PAIR
    sizes = dict(slabs=slabs, blocks=blocks, extra=extra)
    spread_rows, far_rows = slabs * parts * blocks, slabs * parts * extra

    slots = links[:, blocks:, 1]
    named = slots - blocks
    hit = named[:, :, None] == jnp.arange(slabs, dtype=jnp.int32)
    block_named = jnp.sum(jnp.where(hit, wanted[:, None, :], 0), -1)
    is_far = (named >= 0) & (links[:, blocks:, 0] >= 0)
    piece = jnp.where(is_far, named * blocks + block_named, -1).reshape(-1)
    all_pieces = jnp.arange(slabs * blocks, dtype=jnp.int32)
    hot = (piece[:, None] == all_pieces[None, :]).astype(bf)
    hot_turned = (all_pieces[:, None] == piece[None, :]).astype(bf)
    own_links = lax.dynamic_index_in_dim(links, slab_index, 0, keepdims=False)
    link_ids = jnp.arange(link_count, dtype=jnp.int32)
    own_slots = jnp.where(own_links[:, 1] >= blocks, link_ids, own_links[:, 1])
    own_links = jnp.stack([own_links[:, 0], own_slots], -1)

    packed = pl.pallas_call(
        pack_kernel,
        out_shape=jax.ShapeDtypeStruct((blocks, 2 * BLK, PAIR), bf),
        in_specs=[VMEM] * 4,
        out_specs=VMEM,
        compiler_params=params,
        cost_estimate=cost(0, 4 * blocks * tile_bytes),
        name="pack",
    )(queries, keys, values, out_grad)
    near = lax.all_to_all(packed, "head", split_axis=0, concat_axis=0, tiled=True)

    pieces = pl.pallas_call(
        functools.partial(spread_kernel, slabs=slabs),
        out_shape=jax.ShapeDtypeStruct((spread_rows, PAIR), bf),
        in_specs=[VMEM],
        out_specs=VMEM,
        scratch_shapes=[pltpu.VMEM((spread_rows, PAIR), f32)],
        compiler_params=params,
        cost_estimate=cost(0, 2 * blocks * tile_bytes),
        name="spread",
    )(near)
    pieces = lax.all_to_all(pieces, "slab", split_axis=0, concat_axis=0, tiled=True)
    chosen = pl.pallas_call(
        functools.partial(gather_kernel, **sizes),
        out_shape=jax.ShapeDtypeStruct((far_rows, PAIR), bf),
        in_specs=[VMEM, VMEM],
        out_specs=VMEM,
        scratch_shapes=[pltpu.VMEM((far_rows, PAIR), f32)],
        compiler_params=params,
        cost_estimate=cost(2 * far_rows * slabs * blocks * PAIR, 5 * blocks * tile_bytes),
        name="gather",
    )(hot, pieces)
    far = lax.all_to_all(chosen, "slab", split_axis=0, concat_axis=0, tiled=True)

    odq, home, far_out = pl.pallas_call(
        functools.partial(attend_kernel, slabs=slabs),
        out_shape=(
            jax.ShapeDtypeStruct((blocks, *tile), bf),
            jax.ShapeDtypeStruct((blocks, *tile), f32),
            jax.ShapeDtypeStruct((far_rows, PAIR), bf),
        ),
        in_specs=[SMEM, VMEM, VMEM],
        out_specs=(VMEM, VMEM, VMEM),
        scratch_shapes=[
            pltpu.VMEM((link_count, *tile), bf),
            pltpu.VMEM((blocks, 2 * BLK, PAIR), bf),
            pltpu.VMEM((link_count, BLK, BLK), f32),
            pltpu.VMEM((link_count, BLK, BLK), f32),
            pltpu.VMEM((blocks, 1, BLK), f32),
            pltpu.VMEM((blocks, 1, BLK), f32),
            pltpu.VMEM((blocks, 1, BLK), f32),
            pltpu.VMEM((blocks, PAIR, BLK), f32),
            pltpu.VMEM((link_count, *tile), f32),
            pltpu.VMEM((far_rows, PAIR), f32),
        ],
        compiler_params=params,
        cost_estimate=cost(
            link_count * 6 * BLK * BLK * PAIR * 2,
            (2 * extra + 4 * blocks) * tile_bytes,
            link_count * BLK * BLK,
        ),
        name="attend",
    )(own_links, near, far)

    returned = lax.all_to_all(far_out, "slab", split_axis=0, concat_axis=0, tiled=True)
    summed = pl.pallas_call(
        functools.partial(reduce_kernel, **sizes),
        out_shape=jax.ShapeDtypeStruct((spread_rows, PAIR), bf),
        in_specs=[VMEM, VMEM],
        out_specs=VMEM,
        scratch_shapes=[
            pltpu.VMEM((far_rows, PAIR), f32),
            pltpu.VMEM((slabs * extra, parts * PAIR), f32),
        ],
        compiler_params=params,
        cost_estimate=cost(2 * far_rows * slabs * blocks * PAIR, 5 * blocks * tile_bytes),
        name="reduce",
    )(hot_turned, returned)
    summed = lax.all_to_all(summed, "slab", split_axis=0, concat_axis=0, tiled=True)
    results = pl.pallas_call(
        functools.partial(combine_kernel, slabs=slabs),
        out_shape=jax.ShapeDtypeStruct((blocks, 2 * BLK, PAIR), bf),
        in_specs=[VMEM, VMEM, VMEM],
        out_specs=VMEM,
        scratch_shapes=[pltpu.VMEM((spread_rows, PAIR), f32)],
        compiler_params=params,
        cost_estimate=cost(0, 6 * blocks * tile_bytes),
        name="combine",
    )(home, summed, odq)
    mine = lax.all_to_all(results, "head", split_axis=0, concat_axis=0, tiled=True)
    return pl.pallas_call(
        unpack_kernel,
        out_shape=tuple(jax.ShapeDtypeStruct(queries.shape, bf) for _ in range(4)),
        in_specs=[VMEM],
        out_specs=(VMEM,) * 4,
        compiler_params=params,
        cost_estimate=cost(0, 4 * blocks * tile_bytes),
        name="unpack",
    )(mine)


def solution(mesh):
    rows = P(("slab", "head"), None)
    return jax.shard_map(
        body,
        mesh=mesh,
        in_specs=(rows, rows, rows, rows, P(), P()),
        out_specs=(rows,) * 4,
        check_vma=False,
    )
```

```python
import functools
import math

import jax
import jax.numpy as jnp
from jax import lax
from jax.experimental import pallas as pl
from jax.experimental.pallas import tpu as pltpu
from jax.sharding import PartitionSpec as P

HD = 64
BLK = 128
PAIR = 2 * HD
UNROLL = 8
LIMIT = 48 * 1024 * 1024

VMEM = pl.BlockSpec(memory_space=pltpu.VMEM)
SMEM = pl.BlockSpec(memory_space=pltpu.SMEM)
ANY = pl.BlockSpec(memory_space=pl.ANY)


def cost(flops, moved, exps=0):
    return pl.CostEstimate(flops=flops, bytes_accessed=moved, transcendentals=exps)


def pack_kernel(k_ref, v_ref, q_ref, g_ref, kv_ref, qg_ref, held, sems):
    copies = [
        pltpu.make_async_copy(ref, held.at[i], sems.at[i])
        for i, ref in enumerate((k_ref, v_ref, q_ref, g_ref))
    ]
    for copy in copies:
        copy.start()
    for first, out_ref in ((0, kv_ref), (2, qg_ref)):
        copies[first].wait()
        copies[first + 1].wait()
        for h in range(out_ref.shape[0]):
            cols = slice(h * HD, (h + 1) * HD)
            out_ref[h] = jnp.concatenate([held[first, :, cols], held[first + 1, :, cols]], axis=1)


def own_tiles(all_ref, index, held, sems):
    return [
        pltpu.make_async_copy(all_ref.at[i, index], held.at[i], sems.at[i])
        for i in range(held.shape[0])
    ]


def unpack_kernel(index_ref, odq_ref, dkv_ref, o_ref, dq_ref, dk_ref, dv_ref, held, sems):
    copies = own_tiles(odq_ref, index_ref[0], held, sems)
    for copy in copies:
        copy.start()
    for tiles, first_ref, second_ref in ((dkv_ref, dk_ref, dv_ref), (held, dq_ref, o_ref)):
        if tiles is held:
            for copy in copies:
                copy.wait()
        for h in range(0, tiles.shape[0], 2):
            even, odd = tiles[h], tiles[h + 1]
            cols = slice(h * HD, (h + 2) * HD)
            first_ref[:, cols] = jnp.concatenate([even[:, :HD], odd[:, :HD]], axis=1)
            second_ref[:, cols] = jnp.concatenate([even[:, HD:], odd[:, HD:]], axis=1)


def each_piece(slabs, held):
    parts = BLK // slabs
    for c in range(held):
        for part in range(parts):
            yield c, slice(part * slabs, (part + 1) * slabs), pl.ds(
                part * held + c, slabs, stride=parts * held
            )


def spread_kernel(near_ref, out_ref, wide, *, slabs):
    for c, rows, piece_rows in each_piece(slabs, near_ref.shape[0]):
        wide[piece_rows, :] = near_ref[c, rows, :].astype(jnp.float32)
    out_ref[...] = wide[...].astype(jnp.bfloat16)


def gather_kernel(hot_ref, in_ref, out_ref, wide, *, slabs, blocks, extra):
    parts = BLK // slabs
    pieces = in_ref[...].reshape(slabs, parts, blocks, PAIR)
    source = jnp.concatenate(
        [pieces[:, part].reshape(slabs * blocks, PAIR) for part in range(parts)], axis=1
    )
    for t in range(0, slabs, UNROLL):
        picked = jnp.dot(
            hot_ref[t * extra : (t + UNROLL) * extra, :],
            source,
            preferred_element_type=jnp.float32,
        )
        for r in range(UNROLL):
            for part in range(parts):
                start = ((t + r) * parts + part) * extra
                wide[start : start + extra, :] = picked[
                    r * extra : (r + 1) * extra, part * PAIR : (part + 1) * PAIR
                ]
    out_ref[...] = wide[...].astype(jnp.bfloat16)


def reduce_kernel(hot_ref, in_ref, out_ref, wide, beside, *, slabs, blocks, extra):
    parts = BLK // slabs
    wide[...] = in_ref[...].astype(jnp.float32)
    for t in range(slabs):
        for part in range(parts):
            start = (t * parts + part) * extra
            beside[t * extra : (t + 1) * extra, part * PAIR : (part + 1) * PAIR] = wide[
                start : start + extra, :
            ]
    terms = beside[...].astype(jnp.bfloat16)
    for u in range(0, slabs, UNROLL):
        summed = jnp.dot(
            hot_ref[u * blocks : (u + UNROLL) * blocks, :],
            terms,
            preferred_element_type=jnp.float32,
        ).astype(jnp.bfloat16)
        for r in range(UNROLL):
            for part in range(parts):
                start = ((u + r) * parts + part) * blocks
                out_ref[start : start + blocks, :] = summed[
                    r * blocks : (r + 1) * blocks, part * PAIR : (part + 1) * PAIR
                ]


def attend_kernel(
    index_ref,
    links_ref,
    near_ref,
    far_ref,
    all_qg_ref,
    odq_ref,
    home_ref,
    far_out_ref,
    table,
    masked,
    s_buf,
    d_buf,
    top,
    total,
    delta,
    acc,
    dkv,
    wide,
    qg,
    sems,
    *,
    slabs,
):
    copies = own_tiles(all_qg_ref, index_ref[0], qg, sems)
    for copy in copies:
        copy.start()
    blocks, slots = near_ref.shape[0], table.shape[0]
    link_count = links_ref.shape[0]
    score_scale = 1.0 / math.sqrt(HD)
    exp_scale = score_scale * math.log2(math.e)
    left = lax.broadcasted_iota(jnp.int32, (BLK, PAIR), 1) < HD

    wide[...] = far_ref[...].astype(jnp.float32)
    for p, rows, piece_rows in each_piece(slabs, slots - blocks):
        table[blocks + p, rows, :] = wide[piece_rows, :].astype(jnp.bfloat16)
    for b in range(blocks):
        table[b] = near_ref[b]
    top[...] = jnp.full_like(top, -3e38)
    total[...] = jnp.zeros_like(total)
    delta[...] = jnp.zeros_like(delta)
    acc[...] = jnp.zeros_like(acc)
    dkv[...] = jnp.zeros_like(dkv)
    for copy in copies:
        copy.wait()
    for b in range(blocks):
        own = qg[b]
        masked[b, :BLK, :] = jnp.where(left, own, jnp.zeros_like(own))
        masked[b, BLK:, :] = jnp.where(left, jnp.zeros_like(own), own)

    def each_link(step):
        def group(i, _):
            for r in range(UNROLL):
                j = i * UNROLL + r
                queried = links_ref[j, 0]
                step(j, jnp.maximum(queried, 0), links_ref[j, 1], queried >= 0)
            return 0

        lax.fori_loop(0, link_count // UNROLL, group, 0)

    def score_step(j, b, s, valid):
        both = lax.dot_general(
            table[s], masked[b], (((1,), (1,)), ((), ())), preferred_element_type=jnp.float32
        )
        s_buf[j] = both[:, :BLK]
        d_buf[j] = both[:, BLK:]
        largest = jnp.max(both[:, :BLK], axis=0, keepdims=True)
        top[b] = jnp.maximum(top[b], jnp.where(valid, largest, -3e38))

    def sum_step(j, b, s, valid):
        shift = top[b] + jnp.where(valid, 0.0, 1e30)
        raised = jnp.exp2((s_buf[j] - shift) * exp_scale)
        s_buf[j] = raised
        total[b] = total[b] + jnp.sum(raised, axis=0, keepdims=True)
        delta[b] = delta[b] + jnp.sum(raised * d_buf[j], axis=0, keepdims=True)

    def grad_step(j, b, s, valid):
        prob = (s_buf[j] * total[b]).astype(jnp.bfloat16)
        dscore = (prob.astype(jnp.float32) * (d_buf[j] - delta[b]) * score_scale).astype(
            jnp.bfloat16
        )
        turned = lax.dot_general(
            table[s],
            jnp.concatenate([prob, dscore], axis=1),
            (((0,), (0,)), ((), ())),
            preferred_element_type=jnp.float32,
        )
        acc[b, :HD, :] += turned[:HD, BLK:]
        acc[b, HD:, :] += turned[HD:, :BLK]
        terms = jnp.dot(
            jnp.concatenate([dscore, prob], axis=0),
            qg[b],
            preferred_element_type=jnp.float32,
        )
        dkv[s] += jnp.where(left, terms[:BLK], terms[BLK:])

    each_link(score_step)
    each_link(sum_step)
    inverse = 1.0 / total[...]
    delta[...] = delta[...] * inverse
    total[...] = inverse
    each_link(grad_step)

    for p, rows, piece_rows in each_piece(slabs, slots - blocks):
        wide[piece_rows, :] = dkv[blocks + p, rows, :]
    far_out_ref[...] = wide[...].astype(jnp.bfloat16)
    for b in range(blocks):
        odq_ref[b] = acc[b].T.astype(jnp.bfloat16)
    home_ref[...] = dkv[:blocks]


def combine_kernel(home_ref, returned_ref, out_ref, wide, *, slabs):
    wide[...] = returned_ref[...].astype(jnp.float32)
    for c, rows, piece_rows in each_piece(slabs, home_ref.shape[0]):
        out_ref[c, rows, :] = (home_ref[c, rows, :] + wide[piece_rows, :]).astype(jnp.bfloat16)


def body(queries, keys, values, out_grad, links, wanted):
    slabs = lax.axis_size("slab")
    blocks = lax.axis_size("head")
    slab_index = lax.axis_index("slab")
    link_count = links.shape[1]
    extra = link_count - blocks
    parts = BLK // slabs
    bf, f32 = jnp.bfloat16, jnp.float32
    params = pltpu.CompilerParams(vmem_limit_bytes=LIMIT)
    tile = (BLK, PAIR)
    tile_bytes = 2 * BLK * PAIR
    sizes = dict(slabs=slabs, blocks=blocks, extra=extra)
    spread_rows, far_rows = slabs * parts * blocks, slabs * parts * extra

    slots = links[:, blocks:, 1]
    named = slots - blocks
    hit = named[:, :, None] == jnp.arange(slabs, dtype=jnp.int32)
    block_named = jnp.sum(jnp.where(hit, wanted[:, None, :], 0), -1)
    is_far = (named >= 0) & (links[:, blocks:, 0] >= 0)
    piece = jnp.where(is_far, named * blocks + block_named, -1).reshape(-1)
    all_pieces = jnp.arange(slabs * blocks, dtype=jnp.int32)
    hot = (piece[:, None] == all_pieces[None, :]).astype(bf)
    hot_turned = (all_pieces[:, None] == piece[None, :]).astype(bf)
    own_links = lax.dynamic_index_in_dim(links, slab_index, 0, keepdims=False)
    link_ids = jnp.arange(link_count, dtype=jnp.int32)
    own_slots = jnp.where(own_links[:, 1] >= blocks, link_ids, own_links[:, 1])
    own_links = jnp.stack([own_links[:, 0], own_slots], -1)

    own_index = lax.axis_index("head").astype(jnp.int32).reshape(1)
    kv, qg = pl.pallas_call(
        pack_kernel,
        out_shape=(jax.ShapeDtypeStruct((blocks, *tile), bf),) * 2,
        in_specs=[ANY] * 4,
        out_specs=(VMEM,) * 2,
        scratch_shapes=[
            pltpu.VMEM((4, *queries.shape), bf),
            pltpu.SemaphoreType.DMA((4,)),
        ],
        cost_estimate=cost(0, 4 * blocks * tile_bytes),
        name="pack",
    )(keys, values, queries, out_grad)
    near = lax.all_to_all(kv, "head", split_axis=0, concat_axis=0, tiled=True)
    all_qg = lax.all_gather(qg, "head")

    pieces = pl.pallas_call(
        functools.partial(spread_kernel, slabs=slabs),
        out_shape=jax.ShapeDtypeStruct((spread_rows, PAIR), bf),
        in_specs=[VMEM],
        out_specs=VMEM,
        scratch_shapes=[pltpu.VMEM((spread_rows, PAIR), f32)],
        compiler_params=params,
        cost_estimate=cost(0, 2 * blocks * tile_bytes),
        name="spread",
    )(near)
    pieces = lax.all_to_all(pieces, "slab", split_axis=0, concat_axis=0, tiled=True)
    chosen = pl.pallas_call(
        functools.partial(gather_kernel, **sizes),
        out_shape=jax.ShapeDtypeStruct((far_rows, PAIR), bf),
        in_specs=[VMEM, VMEM],
        out_specs=VMEM,
        scratch_shapes=[pltpu.VMEM((far_rows, PAIR), f32)],
        compiler_params=params,
        cost_estimate=cost(2 * far_rows * slabs * blocks * PAIR, 5 * blocks * tile_bytes),
        name="gather",
    )(hot, pieces)
    far = lax.all_to_all(chosen, "slab", split_axis=0, concat_axis=0, tiled=True)

    odq, home, far_out = pl.pallas_call(
        functools.partial(attend_kernel, slabs=slabs),
        out_shape=(
            jax.ShapeDtypeStruct((blocks, *tile), bf),
            jax.ShapeDtypeStruct((blocks, *tile), f32),
            jax.ShapeDtypeStruct((far_rows, PAIR), bf),
        ),
        in_specs=[SMEM, SMEM, VMEM, VMEM, ANY],
        out_specs=(VMEM, VMEM, VMEM),
        scratch_shapes=[
            pltpu.VMEM((link_count, *tile), bf),
            pltpu.VMEM((blocks, 2 * BLK, PAIR), bf),
            pltpu.VMEM((link_count, BLK, BLK), f32),
            pltpu.VMEM((link_count, BLK, BLK), f32),
            pltpu.VMEM((blocks, 1, BLK), f32),
            pltpu.VMEM((blocks, 1, BLK), f32),
            pltpu.VMEM((blocks, 1, BLK), f32),
            pltpu.VMEM((blocks, PAIR, BLK), f32),
            pltpu.VMEM((link_count, *tile), f32),
            pltpu.VMEM((far_rows, PAIR), f32),
            pltpu.VMEM((blocks, *tile), bf),
            pltpu.SemaphoreType.DMA((blocks,)),
        ],
        compiler_params=params,
        cost_estimate=cost(
            link_count * 6 * BLK * BLK * PAIR * 2,
            (2 * extra + 4 * blocks) * tile_bytes,
            link_count * BLK * BLK,
        ),
        name="attend",
    )(own_index, own_links, near, far, all_qg)
    all_odq = lax.all_gather(odq, "head")

    returned = lax.all_to_all(far_out, "slab", split_axis=0, concat_axis=0, tiled=True)
    summed = pl.pallas_call(
        functools.partial(reduce_kernel, **sizes),
        out_shape=jax.ShapeDtypeStruct((spread_rows, PAIR), bf),
        in_specs=[VMEM, VMEM],
        out_specs=VMEM,
        scratch_shapes=[
            pltpu.VMEM((far_rows, PAIR), f32),
            pltpu.VMEM((slabs * extra, parts * PAIR), f32),
        ],
        compiler_params=params,
        cost_estimate=cost(2 * far_rows * slabs * blocks * PAIR, 5 * blocks * tile_bytes),
        name="reduce",
    )(hot_turned, returned)
    summed = lax.all_to_all(summed, "slab", split_axis=0, concat_axis=0, tiled=True)
    dkv = pl.pallas_call(
        functools.partial(combine_kernel, slabs=slabs),
        out_shape=jax.ShapeDtypeStruct((blocks, *tile), bf),
        in_specs=[VMEM, VMEM],
        out_specs=VMEM,
        scratch_shapes=[pltpu.VMEM((spread_rows, PAIR), f32)],
        compiler_params=params,
        cost_estimate=cost(0, 5 * blocks * tile_bytes),
        name="combine",
    )(home, summed)
    dkv = lax.all_to_all(dkv, "head", split_axis=0, concat_axis=0, tiled=True)
    return pl.pallas_call(
        unpack_kernel,
        out_shape=tuple(jax.ShapeDtypeStruct(queries.shape, bf) for _ in range(4)),
        in_specs=[SMEM, ANY, VMEM],
        out_specs=(VMEM,) * 4,
        scratch_shapes=[
            pltpu.VMEM((blocks, *tile), bf),
            pltpu.SemaphoreType.DMA((blocks,)),
        ],
        cost_estimate=cost(0, 4 * blocks * tile_bytes),
        name="unpack",
    )(own_index, all_odq, dkv)


def solution(mesh):
    rows = P(("slab", "head"), None)
    return jax.shard_map(
        body,
        mesh=mesh,
        in_specs=(rows, rows, rows, rows, P(), P()),
        out_specs=(rows,) * 4,
        check_vma=False,
    )
```

```python
import functools
import math

import jax
import jax.numpy as jnp
from jax import lax
from jax.experimental import pallas as pl
from jax.experimental.pallas import tpu as pltpu
from jax.sharding import PartitionSpec as P

HD = 64
BLK = 128
PAIR = 2 * HD
UNROLL = 8
FEW = 16
LIMIT = 48 * 1024 * 1024

VMEM = pl.BlockSpec(memory_space=pltpu.VMEM)
SMEM = pl.BlockSpec(memory_space=pltpu.SMEM)
ANY = pl.BlockSpec(memory_space=pl.ANY)


def cost(flops, moved, exps=0):
    return pl.CostEstimate(flops=flops, bytes_accessed=moved, transcendentals=exps)


def pack_kernel(k_ref, v_ref, q_ref, g_ref, kv_ref, qg_ref, held, sems):
    copies = [
        pltpu.make_async_copy(ref, held.at[i], sems.at[i])
        for i, ref in enumerate((k_ref, v_ref, q_ref, g_ref))
    ]
    for copy in copies:
        copy.start()
    for first, out_ref in ((0, kv_ref), (2, qg_ref)):
        copies[first].wait()
        copies[first + 1].wait()
        for h in range(out_ref.shape[0]):
            cols = slice(h * HD, (h + 1) * HD)
            out_ref[h] = jnp.concatenate([held[first, :, cols], held[first + 1, :, cols]], axis=1)


def own_tiles(all_ref, index, held, sems):
    return [
        pltpu.make_async_copy(all_ref.at[i, index], held.at[i], sems.at[i])
        for i in range(held.shape[0])
    ]


def unpack_kernel(index_ref, odq_ref, dkv_ref, o_ref, dq_ref, dk_ref, dv_ref, held, sems):
    copies = own_tiles(odq_ref, index_ref[0], held, sems)
    for copy in copies:
        copy.start()
    for tiles, first_ref, second_ref in ((dkv_ref, dk_ref, dv_ref), (held, dq_ref, o_ref)):
        if tiles is held:
            for copy in copies:
                copy.wait()
        for h in range(0, tiles.shape[0], 2):
            even, odd = tiles[h], tiles[h + 1]
            cols = slice(h * HD, (h + 2) * HD)
            first_ref[:, cols] = jnp.concatenate([even[:, :HD], odd[:, :HD]], axis=1)
            second_ref[:, cols] = jnp.concatenate([even[:, HD:], odd[:, HD:]], axis=1)


def each_piece(slabs, held):
    parts = BLK // slabs
    for c in range(held):
        for part in range(parts):
            yield c, slice(part * slabs, (part + 1) * slabs), pl.ds(
                part * held + c, slabs, stride=parts * held
            )


def spread_kernel(near_ref, out_ref, wide, *, slabs):
    for c, rows, piece_rows in each_piece(slabs, near_ref.shape[0]):
        wide[piece_rows, :] = near_ref[c, rows, :].astype(jnp.float32)
    out_ref[...] = wide[...].astype(jnp.bfloat16)


def gather_kernel(hot_ref, in_ref, out_ref, wide, *, slabs, blocks, extra):
    parts = BLK // slabs
    pieces = in_ref[...].reshape(slabs, parts, blocks, PAIR)
    source = jnp.concatenate(
        [pieces[:, part].reshape(slabs * blocks, PAIR) for part in range(parts)], axis=1
    )
    for t in range(0, slabs, UNROLL):
        picked = jnp.dot(
            hot_ref[t * extra : (t + UNROLL) * extra, :],
            source,
            preferred_element_type=jnp.float32,
        )
        for r in range(UNROLL):
            for part in range(parts):
                start = ((t + r) * parts + part) * extra
                wide[start : start + extra, :] = picked[
                    r * extra : (r + 1) * extra, part * PAIR : (part + 1) * PAIR
                ]
    out_ref[...] = wide[...].astype(jnp.bfloat16)


def reduce_kernel(hot_ref, in_ref, out_ref, wide, beside, *, slabs, blocks, extra):
    parts = BLK // slabs
    wide[...] = in_ref[...].astype(jnp.float32)
    for t in range(slabs):
        for part in range(parts):
            start = (t * parts + part) * extra
            beside[t * extra : (t + 1) * extra, part * PAIR : (part + 1) * PAIR] = wide[
                start : start + extra, :
            ]
    terms = beside[...].astype(jnp.bfloat16)
    for u in range(0, slabs, UNROLL):
        summed = jnp.dot(
            hot_ref[u * blocks : (u + UNROLL) * blocks, :],
            terms,
            preferred_element_type=jnp.float32,
        ).astype(jnp.bfloat16)
        for r in range(UNROLL):
            for part in range(parts):
                start = ((u + r) * parts + part) * blocks
                out_ref[start : start + blocks, :] = summed[
                    r * blocks : (r + 1) * blocks, part * PAIR : (part + 1) * PAIR
                ]


def attend_kernel(
    index_ref,
    links_ref,
    near_ref,
    far_ref,
    all_qg_ref,
    odq_ref,
    home_ref,
    far_out_ref,
    table,
    masked,
    s_buf,
    d_buf,
    top,
    total,
    delta,
    acc,
    dkv,
    wide,
    qg,
    sems,
    *,
    slabs,
):
    copies = own_tiles(all_qg_ref, index_ref[0], qg, sems)
    for copy in copies:
        copy.start()
    blocks, slots = near_ref.shape[0], table.shape[0]
    link_count = links_ref.shape[0]
    score_scale = 1.0 / math.sqrt(HD)
    exp_scale = score_scale * math.log2(math.e)
    left = lax.broadcasted_iota(jnp.int32, (BLK, PAIR), 1) < HD

    wide[...] = far_ref[...].astype(jnp.float32)
    for p, rows, piece_rows in each_piece(slabs, slots - blocks):
        table[blocks + p, rows, :] = wide[piece_rows, :].astype(jnp.bfloat16)
    for b in range(blocks):
        table[b] = near_ref[b]
    top[...] = jnp.full_like(top, -3e38)
    total[...] = jnp.zeros_like(total)
    delta[...] = jnp.zeros_like(delta)
    acc[...] = jnp.zeros_like(acc)
    dkv[...] = jnp.zeros_like(dkv)
    for copy in copies:
        copy.wait()
    for b in range(blocks):
        own = qg[b]
        masked[b, :BLK, :] = jnp.where(left, own, jnp.zeros_like(own))
        masked[b, BLK:, :] = jnp.where(left, jnp.zeros_like(own), own)

    def each_link(step):
        def group(i, _):
            for r in range(UNROLL):
                j = i * UNROLL + r
                queried = links_ref[j, 0]
                step(j, jnp.maximum(queried, 0), links_ref[j, 1], queried >= 0)
            return 0

        lax.fori_loop(0, link_count // UNROLL, group, 0)

    def score_step(j, b, s, valid):
        both = lax.dot_general(
            table[s], masked[b], (((1,), (1,)), ((), ())), preferred_element_type=jnp.float32
        )
        s_buf[j] = both[:, :BLK]
        d_buf[j] = both[:, BLK:]
        largest = jnp.max(both[:, :BLK], axis=0, keepdims=True)
        top[b] = jnp.maximum(top[b], jnp.where(valid, largest, -3e38))

    def sum_step(j, b, s, valid):
        shift = top[b] + jnp.where(valid, 0.0, 1e30)
        raised = jnp.exp2((s_buf[j] - shift) * exp_scale)
        s_buf[j] = raised
        total[b] = total[b] + jnp.sum(raised, axis=0, keepdims=True)
        delta[b] = delta[b] + jnp.sum(raised * d_buf[j], axis=0, keepdims=True)

    def grad_step(j, b, s, valid):
        prob = (s_buf[j] * total[b]).astype(jnp.bfloat16)
        dscore = (prob.astype(jnp.float32) * (d_buf[j] - delta[b]) * score_scale).astype(
            jnp.bfloat16
        )
        turned = lax.dot_general(
            table[s],
            jnp.concatenate([prob, dscore], axis=1),
            (((0,), (0,)), ((), ())),
            preferred_element_type=jnp.float32,
        )
        acc[b, :HD, :] += turned[:HD, BLK:]
        acc[b, HD:, :] += turned[HD:, :BLK]
        terms = jnp.dot(
            jnp.concatenate([dscore, prob], axis=0),
            qg[b],
            preferred_element_type=jnp.float32,
        )
        dkv[s] += jnp.where(left, terms[:BLK], terms[BLK:])

    each_link(score_step)
    each_link(sum_step)
    inverse = 1.0 / total[...]
    delta[...] = delta[...] * inverse
    total[...] = inverse
    each_link(grad_step)

    for p, rows, piece_rows in each_piece(slabs, slots - blocks):
        wide[piece_rows, :] = dkv[blocks + p, rows, :]
    far_out_ref[...] = wide[...].astype(jnp.bfloat16)
    for b in range(blocks):
        odq_ref[b] = acc[b].T.astype(jnp.bfloat16)
    home_ref[...] = dkv[:blocks]


def combine_kernel(home_ref, returned_ref, out_ref, wide, *, slabs):
    wide[...] = returned_ref[...].astype(jnp.float32)
    for c, rows, piece_rows in each_piece(slabs, home_ref.shape[0]):
        out_ref[c, rows, :] = (home_ref[c, rows, :] + wide[piece_rows, :]).astype(jnp.bfloat16)


def body(queries, keys, values, out_grad, links, wanted):
    slabs = lax.axis_size("slab")
    blocks = lax.axis_size("head")
    extra = links.shape[1] - blocks
    named = links[:, blocks:, 1] - blocks
    hit = named[:, :, None] == jnp.arange(slabs, dtype=jnp.int32)
    used = jnp.any(hit & (links[:, blocks:, :1] >= 0), 1)
    most = jnp.max(jnp.sum(used.astype(jnp.int32), 1))
    given = (queries, keys, values, out_grad, used, links, wanted)
    if extra <= FEW:
        return step(*given, extra=extra)
    return lax.cond(
        most <= FEW,
        functools.partial(step, extra=FEW),
        functools.partial(step, extra=extra),
        *given,
    )


def step(queries, keys, values, out_grad, used, links, wanted, *, extra):
    slabs = lax.axis_size("slab")
    blocks = lax.axis_size("head")
    slab_index = lax.axis_index("slab")
    link_count = links.shape[1]
    parts = BLK // slabs
    bf, f32 = jnp.bfloat16, jnp.float32
    params = pltpu.CompilerParams(vmem_limit_bytes=LIMIT)
    tile = (BLK, PAIR)
    tile_bytes = 2 * BLK * PAIR
    sizes = dict(slabs=slabs, blocks=blocks, extra=extra)
    spread_rows, far_rows = slabs * parts * blocks, slabs * parts * extra

    slab_ids = jnp.arange(slabs, dtype=jnp.int32)
    before = (slab_ids[:, None] < slab_ids[None, :]).astype(bf)
    place = jnp.dot(used.astype(bf), before, preferred_element_type=f32).astype(jnp.int32)
    places = jnp.arange(extra, dtype=jnp.int32)
    at = used[:, None, :] & (place[:, None, :] == places[None, :, None])
    row = slab_ids[None, :] * blocks + wanted
    piece = jnp.sum(jnp.where(at, row[:, None, :] + 1, 0), -1).reshape(-1) - 1
    all_pieces = jnp.arange(slabs * blocks, dtype=jnp.int32)
    hot = (piece[:, None] == all_pieces[None, :]).astype(bf)
    hot_turned = (all_pieces[:, None] == piece[None, :]).astype(bf)
    own_links = lax.dynamic_index_in_dim(links, slab_index, 0, keepdims=False)
    own_place = lax.dynamic_index_in_dim(place, slab_index, 0, keepdims=False)
    own_named = own_links[:, 1] - blocks
    own_place = jnp.sum(jnp.where(own_named[:, None] == slab_ids, own_place, 0), -1)
    own_slots = jnp.where(
        own_named >= 0, blocks + jnp.minimum(own_place, extra - 1), own_links[:, 1]
    )
    own_links = jnp.stack([own_links[:, 0], own_slots], -1)

    own_index = lax.axis_index("head").astype(jnp.int32).reshape(1)
    kv, qg = pl.pallas_call(
        pack_kernel,
        out_shape=(jax.ShapeDtypeStruct((blocks, *tile), bf),) * 2,
        in_specs=[ANY] * 4,
        out_specs=(VMEM,) * 2,
        scratch_shapes=[
            pltpu.VMEM((4, *queries.shape), bf),
            pltpu.SemaphoreType.DMA((4,)),
        ],
        cost_estimate=cost(0, 4 * blocks * tile_bytes),
        name="pack",
    )(keys, values, queries, out_grad)
    near = lax.all_to_all(kv, "head", split_axis=0, concat_axis=0, tiled=True)
    all_qg = lax.all_gather(qg, "head")

    pieces = pl.pallas_call(
        functools.partial(spread_kernel, slabs=slabs),
        out_shape=jax.ShapeDtypeStruct((spread_rows, PAIR), bf),
        in_specs=[VMEM],
        out_specs=VMEM,
        scratch_shapes=[pltpu.VMEM((spread_rows, PAIR), f32)],
        compiler_params=params,
        cost_estimate=cost(0, 2 * blocks * tile_bytes),
        name="spread",
    )(near)
    pieces = lax.all_to_all(pieces, "slab", split_axis=0, concat_axis=0, tiled=True)
    chosen = pl.pallas_call(
        functools.partial(gather_kernel, **sizes),
        out_shape=jax.ShapeDtypeStruct((far_rows, PAIR), bf),
        in_specs=[VMEM, VMEM],
        out_specs=VMEM,
        scratch_shapes=[pltpu.VMEM((far_rows, PAIR), f32)],
        compiler_params=params,
        cost_estimate=cost(2 * far_rows * slabs * blocks * PAIR, 5 * blocks * tile_bytes),
        name="gather",
    )(hot, pieces)
    far = lax.all_to_all(chosen, "slab", split_axis=0, concat_axis=0, tiled=True)

    odq, home, far_out = pl.pallas_call(
        functools.partial(attend_kernel, slabs=slabs),
        out_shape=(
            jax.ShapeDtypeStruct((blocks, *tile), bf),
            jax.ShapeDtypeStruct((blocks, *tile), f32),
            jax.ShapeDtypeStruct((far_rows, PAIR), bf),
        ),
        in_specs=[SMEM, SMEM, VMEM, VMEM, ANY],
        out_specs=(VMEM, VMEM, VMEM),
        scratch_shapes=[
            pltpu.VMEM((blocks + extra, *tile), bf),
            pltpu.VMEM((blocks, 2 * BLK, PAIR), bf),
            pltpu.VMEM((link_count, BLK, BLK), f32),
            pltpu.VMEM((link_count, BLK, BLK), f32),
            pltpu.VMEM((blocks, 1, BLK), f32),
            pltpu.VMEM((blocks, 1, BLK), f32),
            pltpu.VMEM((blocks, 1, BLK), f32),
            pltpu.VMEM((blocks, PAIR, BLK), f32),
            pltpu.VMEM((blocks + extra, *tile), f32),
            pltpu.VMEM((far_rows, PAIR), f32),
            pltpu.VMEM((blocks, *tile), bf),
            pltpu.SemaphoreType.DMA((blocks,)),
        ],
        compiler_params=params,
        cost_estimate=cost(
            link_count * 6 * BLK * BLK * PAIR * 2,
            (2 * extra + 4 * blocks) * tile_bytes,
            link_count * BLK * BLK,
        ),
        name="attend",
    )(own_index, own_links, near, far, all_qg)
    all_odq = lax.all_gather(odq, "head")

    returned = lax.all_to_all(far_out, "slab", split_axis=0, concat_axis=0, tiled=True)
    summed = pl.pallas_call(
        functools.partial(reduce_kernel, **sizes),
        out_shape=jax.ShapeDtypeStruct((spread_rows, PAIR), bf),
        in_specs=[VMEM, VMEM],
        out_specs=VMEM,
        scratch_shapes=[
            pltpu.VMEM((far_rows, PAIR), f32),
            pltpu.VMEM((slabs * extra, parts * PAIR), f32),
        ],
        compiler_params=params,
        cost_estimate=cost(2 * far_rows * slabs * blocks * PAIR, 5 * blocks * tile_bytes),
        name="reduce",
    )(hot_turned, returned)
    summed = lax.all_to_all(summed, "slab", split_axis=0, concat_axis=0, tiled=True)
    dkv = pl.pallas_call(
        functools.partial(combine_kernel, slabs=slabs),
        out_shape=jax.ShapeDtypeStruct((blocks, *tile), bf),
        in_specs=[VMEM, VMEM],
        out_specs=VMEM,
        scratch_shapes=[pltpu.VMEM((spread_rows, PAIR), f32)],
        compiler_params=params,
        cost_estimate=cost(0, 5 * blocks * tile_bytes),
        name="combine",
    )(home, summed)
    dkv = lax.all_to_all(dkv, "head", split_axis=0, concat_axis=0, tiled=True)
    return pl.pallas_call(
        unpack_kernel,
        out_shape=tuple(jax.ShapeDtypeStruct(queries.shape, bf) for _ in range(4)),
        in_specs=[SMEM, ANY, VMEM],
        out_specs=(VMEM,) * 4,
        scratch_shapes=[
            pltpu.VMEM((blocks, *tile), bf),
            pltpu.SemaphoreType.DMA((blocks,)),
        ],
        cost_estimate=cost(0, 4 * blocks * tile_bytes),
        name="unpack",
    )(own_index, all_odq, dkv)


def solution(mesh):
    rows = P(("slab", "head"), None)
    return jax.shard_map(
        body,
        mesh=mesh,
        in_specs=(rows, rows, rows, rows, P(), P()),
        out_specs=(rows,) * 4,
        check_vma=False,
    )
```

```python
import functools
import math

import jax
import jax.numpy as jnp
from jax import lax
from jax.experimental import pallas as pl
from jax.experimental.pallas import tpu as pltpu
from jax.sharding import PartitionSpec as P

HD = 64
BLK = 128
PAIR = 2 * HD
UNROLL = 8
OTHER_UNROLL = 12
FEW = 16
LIMIT = 48 * 1024 * 1024
ATTEND_LIMIT = 60 * 1024 * 1024

VMEM = pl.BlockSpec(memory_space=pltpu.VMEM)
SMEM = pl.BlockSpec(memory_space=pltpu.SMEM)
ANY = pl.BlockSpec(memory_space=pl.ANY)


def cost(flops, moved, exps=0):
    return pl.CostEstimate(flops=flops, bytes_accessed=moved, transcendentals=exps)


def most_far(links_ref, blocks):
    queried, slots = links_ref[blocks:, 0, :], links_ref[blocks:, 1, :]
    order = lax.broadcasted_iota(jnp.int32, slots.shape, 0)
    far = (queried >= 0) & (slots >= blocks)
    keys = jnp.where(far, slots, -1 - order)
    total = far[:1].astype(jnp.float32)
    for p in range(1, slots.shape[0]):
        same = (keys[:p] == keys[p : p + 1]).astype(jnp.float32)
        again = jnp.max(same, axis=0, keepdims=True)
        total = total + far[p : p + 1].astype(jnp.float32) * (1.0 - again)
    return jnp.max(total).astype(jnp.int32)


def pack_kernel(links_ref, k_ref, v_ref, q_ref, g_ref, kv_ref, qg_ref, most_ref, held, sems):
    copies = [
        pltpu.make_async_copy(ref, held.at[i], sems.at[i])
        for i, ref in enumerate((k_ref, v_ref, q_ref, g_ref))
    ]
    for copy in copies:
        copy.start()
    most_ref[0] = most_far(links_ref, kv_ref.shape[0])
    for first, out_ref in ((0, kv_ref), (2, qg_ref)):
        copies[first].wait()
        copies[first + 1].wait()
        for h in range(out_ref.shape[0]):
            cols = slice(h * HD, (h + 1) * HD)
            out_ref[h] = jnp.concatenate([held[first, :, cols], held[first + 1, :, cols]], axis=1)


def own_tiles(all_ref, index, held, sems):
    return [
        pltpu.make_async_copy(all_ref.at[i, index], held.at[i], sems.at[i])
        for i in range(held.shape[0])
    ]


def unpack_kernel(
    index_ref, odq_ref, dkv_ref, o_ref, dq_ref, dk_ref, dv_ref, held, rows, sems, out_sems
):
    copies = own_tiles(odq_ref, index_ref[0], held, sems)
    for copy in copies:
        copy.start()
    outs = []
    for tiles, first, out_refs in ((dkv_ref, 0, (dk_ref, dv_ref)), (held, 2, (dq_ref, o_ref))):
        if tiles is held:
            for copy in copies:
                copy.wait()
        for h in range(0, tiles.shape[0], 2):
            even, odd = tiles[h], tiles[h + 1]
            cols = slice(h * HD, (h + 2) * HD)
            rows[first, :, cols] = jnp.concatenate([even[:, :HD], odd[:, :HD]], axis=1)
            rows[first + 1, :, cols] = jnp.concatenate([even[:, HD:], odd[:, HD:]], axis=1)
        for i, out_ref in enumerate(out_refs, first):
            outs.append(pltpu.make_async_copy(rows.at[i], out_ref, out_sems.at[i]))
            outs[-1].start()
    for out in outs:
        out.wait()


def each_piece(slabs, held):
    parts = BLK // slabs
    for c in range(held):
        for part in range(parts):
            yield c, slice(part * slabs, (part + 1) * slabs), pl.ds(
                part * held + c, slabs, stride=parts * held
            )


def spread_kernel(near_ref, out_ref, wide, *, slabs):
    for c, rows, piece_rows in each_piece(slabs, near_ref.shape[0]):
        wide[piece_rows, :] = near_ref[c, rows, :].astype(jnp.float32)
    out_ref[...] = wide[...].astype(jnp.bfloat16)


def gather_kernel(hot_ref, in_ref, out_ref, wide, *, slabs, blocks, extra):
    parts = BLK // slabs
    pieces = in_ref[...].reshape(slabs, parts, blocks, PAIR)
    source = jnp.concatenate(
        [pieces[:, part].reshape(slabs * blocks, PAIR) for part in range(parts)], axis=1
    )
    for t in range(0, slabs, UNROLL):
        picked = jnp.dot(
            hot_ref[t * extra : (t + UNROLL) * extra, :],
            source,
            preferred_element_type=jnp.float32,
        )
        for r in range(UNROLL):
            for part in range(parts):
                start = ((t + r) * parts + part) * extra
                wide[start : start + extra, :] = picked[
                    r * extra : (r + 1) * extra, part * PAIR : (part + 1) * PAIR
                ]
    out_ref[...] = wide[...].astype(jnp.bfloat16)


def reduce_kernel(hot_ref, in_ref, out_ref, wide, beside, *, slabs, blocks, extra):
    parts = BLK // slabs
    wide[...] = in_ref[...].astype(jnp.float32)
    for t in range(slabs):
        for part in range(parts):
            start = (t * parts + part) * extra
            beside[t * extra : (t + 1) * extra, part * PAIR : (part + 1) * PAIR] = wide[
                start : start + extra, :
            ]
    terms = beside[...].astype(jnp.bfloat16)
    for u in range(0, slabs, UNROLL):
        summed = jnp.dot(
            hot_ref[u * blocks : (u + UNROLL) * blocks, :],
            terms,
            preferred_element_type=jnp.float32,
        ).astype(jnp.bfloat16)
        for r in range(UNROLL):
            for part in range(parts):
                start = ((u + r) * parts + part) * blocks
                out_ref[start : start + blocks, :] = summed[
                    r * blocks : (r + 1) * blocks, part * PAIR : (part + 1) * PAIR
                ]


def attend_kernel(
    index_ref,
    links_ref,
    near_ref,
    far_ref,
    all_qg_ref,
    odq_ref,
    home_ref,
    far_out_ref,
    table,
    masked,
    s_buf,
    d_buf,
    top,
    total,
    delta,
    acc,
    dkv,
    wide,
    qg,
    sems,
    *,
    slabs,
):
    copies = own_tiles(all_qg_ref, index_ref[0], qg, sems)
    for copy in copies:
        copy.start()
    blocks, slots = near_ref.shape[0], table.shape[0]
    link_count = links_ref.shape[0]
    score_scale = 1.0 / math.sqrt(HD)
    exp_scale = score_scale * math.log2(math.e)
    left = lax.broadcasted_iota(jnp.int32, (BLK, PAIR), 1) < HD

    wide[...] = far_ref[...].astype(jnp.float32)
    for p, rows, piece_rows in each_piece(slabs, slots - blocks):
        table[blocks + p, rows, :] = wide[piece_rows, :].astype(jnp.bfloat16)
    for b in range(blocks):
        table[b] = near_ref[b]
    dkv[blocks:] = jnp.zeros((slots - blocks, BLK, PAIR), jnp.float32)
    for copy in copies:
        copy.wait()
    for b in range(blocks):
        own = qg[b]
        masked[b, :BLK, :] = jnp.where(left, own, jnp.zeros_like(own))
        masked[b, BLK:, :] = jnp.where(left, jnp.zeros_like(own), own)

    def each_link(step):
        def other(i, _):
            for r in range(OTHER_UNROLL):
                j = blocks + i * OTHER_UNROLL + r
                queried = links_ref[j, 0]
                step(j, jnp.maximum(queried, 0), links_ref[j, 1], queried >= 0)
            return 0

        for b in range(blocks):
            step(b, b, b, None)
        lax.fori_loop(0, (link_count - blocks) // OTHER_UNROLL, other, 0)

    def score_step(j, b, s, valid):
        both = lax.dot_general(
            table[s], masked[b], (((1,), (1,)), ((), ())), preferred_element_type=jnp.float32
        )
        s_buf[j] = both[:, :BLK]
        d_buf[j] = both[:, BLK:]
        largest = jnp.max(both[:, :BLK], axis=0, keepdims=True)
        if valid is None:
            top[b] = largest
        else:
            top[b] = jnp.maximum(top[b], jnp.where(valid, largest, -3e38))

    def sum_step(j, b, s, valid):
        shift = top[b] if valid is None else top[b] + jnp.where(valid, 0.0, 1e30)
        raised = jnp.exp2((s_buf[j] - shift) * exp_scale)
        s_buf[j] = raised
        part = jnp.sum(raised, axis=0, keepdims=True)
        weighted = jnp.sum(raised * d_buf[j], axis=0, keepdims=True)
        total[b] = part if valid is None else total[b] + part
        delta[b] = weighted if valid is None else delta[b] + weighted

    def grad_step(j, b, s, valid):
        prob = (s_buf[j] * total[b]).astype(jnp.bfloat16)
        dscore = (prob.astype(jnp.float32) * (d_buf[j] - delta[b]) * score_scale).astype(
            jnp.bfloat16
        )
        turned = lax.dot_general(
            table[s],
            jnp.concatenate([prob, dscore], axis=1),
            (((0,), (0,)), ((), ())),
            preferred_element_type=jnp.float32,
        )
        terms = jnp.dot(
            jnp.concatenate([dscore, prob], axis=0),
            qg[b],
            preferred_element_type=jnp.float32,
        )
        both = jnp.where(left, terms[:BLK], terms[BLK:])
        if valid is None:
            acc[b, :HD, :] = turned[:HD, BLK:]
            acc[b, HD:, :] = turned[HD:, :BLK]
            dkv[s] = both
        else:
            acc[b, :HD, :] += turned[:HD, BLK:]
            acc[b, HD:, :] += turned[HD:, :BLK]
            dkv[s] += both

    each_link(score_step)
    each_link(sum_step)
    inverse = 1.0 / total[...]
    delta[...] = delta[...] * inverse
    total[...] = inverse
    each_link(grad_step)

    for p, rows, piece_rows in each_piece(slabs, slots - blocks):
        wide[piece_rows, :] = dkv[blocks + p, rows, :]
    far_out_ref[...] = wide[...].astype(jnp.bfloat16)
    for b in range(blocks):
        odq_ref[b] = acc[b].T.astype(jnp.bfloat16)
    home_ref[...] = dkv[:blocks]


def combine_kernel(home_ref, returned_ref, out_ref, wide, home, sem, *, slabs):
    copy = pltpu.make_async_copy(home_ref, home, sem)
    copy.start()
    wide[...] = returned_ref[...].astype(jnp.float32)
    copy.wait()
    for c, rows, piece_rows in each_piece(slabs, home.shape[0]):
        out_ref[c, rows, :] = (home[c, rows, :] + wide[piece_rows, :]).astype(jnp.bfloat16)


def body(queries, keys, values, out_grad, links, wanted):
    blocks = lax.axis_size("head")
    extra = links.shape[1] - blocks
    bf = jnp.bfloat16
    kv, qg, most = pl.pallas_call(
        pack_kernel,
        out_shape=(
            jax.ShapeDtypeStruct((blocks, BLK, PAIR), bf),
            jax.ShapeDtypeStruct((blocks, BLK, PAIR), bf),
            jax.ShapeDtypeStruct((1,), jnp.int32),
        ),
        in_specs=[VMEM] + [ANY] * 4,
        out_specs=(VMEM, VMEM, SMEM),
        scratch_shapes=[
            pltpu.VMEM((4, *queries.shape), bf),
            pltpu.SemaphoreType.DMA((4,)),
        ],
        cost_estimate=cost(0, 16 * blocks * BLK * PAIR),
        name="pack",
    )(links.transpose(1, 2, 0), keys, values, queries, out_grad)
    given = (kv, qg, links, wanted)
    if extra <= FEW:
        return step(*given, extra=extra)
    return lax.cond(
        most[0] <= FEW,
        functools.partial(step, extra=FEW),
        functools.partial(step, extra=extra),
        *given,
    )


def step(kv, qg, links, wanted, *, extra):
    slabs = lax.axis_size("slab")
    blocks = lax.axis_size("head")
    slab_index = lax.axis_index("slab")
    own_index = lax.axis_index("head").astype(jnp.int32).reshape(1)
    link_count = links.shape[1]
    parts = BLK // slabs
    bf, f32 = jnp.bfloat16, jnp.float32
    params = pltpu.CompilerParams(vmem_limit_bytes=LIMIT)
    tile = (BLK, PAIR)
    tile_bytes = 2 * BLK * PAIR
    sizes = dict(slabs=slabs, blocks=blocks, extra=extra)
    spread_rows, far_rows = slabs * parts * blocks, slabs * parts * extra

    named = links[:, blocks:, 1] - blocks
    hit = named[:, :, None] == jnp.arange(slabs, dtype=jnp.int32)
    used = jnp.any(hit & (links[:, blocks:, :1] >= 0), 1)
    slab_ids = jnp.arange(slabs, dtype=jnp.int32)
    before = (slab_ids[:, None] < slab_ids[None, :]).astype(bf)
    place = jnp.dot(used.astype(bf), before, preferred_element_type=f32).astype(jnp.int32)
    places = jnp.arange(extra, dtype=jnp.int32)
    at = used[:, None, :] & (place[:, None, :] == places[None, :, None])
    row = slab_ids[None, :] * blocks + wanted
    piece = jnp.sum(jnp.where(at, row[:, None, :] + 1, 0), -1).reshape(-1) - 1
    all_pieces = jnp.arange(slabs * blocks, dtype=jnp.int32)
    hot = (piece[:, None] == all_pieces[None, :]).astype(bf)
    own_links = lax.dynamic_index_in_dim(links, slab_index, 0, keepdims=False)
    own_place = lax.dynamic_index_in_dim(place, slab_index, 0, keepdims=False)
    own_named = own_links[:, 1] - blocks
    own_place = jnp.sum(jnp.where(own_named[:, None] == slab_ids, own_place, 0), -1)
    own_slots = jnp.where(
        own_named >= 0, blocks + jnp.minimum(own_place, extra - 1), own_links[:, 1]
    )
    own_links = jnp.stack([own_links[:, 0], own_slots], -1)

    near = lax.all_to_all(kv, "head", split_axis=0, concat_axis=0, tiled=True)
    all_qg = lax.all_gather(qg, "head")

    pieces = pl.pallas_call(
        functools.partial(spread_kernel, slabs=slabs),
        out_shape=jax.ShapeDtypeStruct((spread_rows, PAIR), bf),
        in_specs=[VMEM],
        out_specs=VMEM,
        scratch_shapes=[pltpu.VMEM((spread_rows, PAIR), f32)],
        compiler_params=params,
        cost_estimate=cost(0, 2 * blocks * tile_bytes),
        name="spread",
    )(near)
    pieces = lax.all_to_all(pieces, "slab", split_axis=0, concat_axis=0, tiled=True)
    pieces, own_links = lax.optimization_barrier((pieces, own_links))
    chosen = pl.pallas_call(
        functools.partial(gather_kernel, **sizes),
        out_shape=jax.ShapeDtypeStruct((far_rows, PAIR), bf),
        in_specs=[VMEM, VMEM],
        out_specs=VMEM,
        scratch_shapes=[pltpu.VMEM((far_rows, PAIR), f32)],
        compiler_params=params,
        cost_estimate=cost(2 * far_rows * slabs * blocks * PAIR, 5 * blocks * tile_bytes),
        name="gather",
    )(hot, pieces)
    far = lax.all_to_all(chosen, "slab", split_axis=0, concat_axis=0, tiled=True)

    odq, home, far_out = pl.pallas_call(
        functools.partial(attend_kernel, slabs=slabs),
        out_shape=(
            jax.ShapeDtypeStruct((blocks, *tile), bf),
            jax.ShapeDtypeStruct((blocks, *tile), f32),
            jax.ShapeDtypeStruct((far_rows, PAIR), bf),
        ),
        in_specs=[SMEM, SMEM, VMEM, VMEM, ANY],
        out_specs=(VMEM, VMEM, VMEM),
        scratch_shapes=[
            pltpu.VMEM((blocks + extra, *tile), bf),
            pltpu.VMEM((blocks, 2 * BLK, PAIR), bf),
            pltpu.VMEM((link_count, BLK, BLK), f32),
            pltpu.VMEM((link_count, BLK, BLK), f32),
            pltpu.VMEM((blocks, 1, BLK), f32),
            pltpu.VMEM((blocks, 1, BLK), f32),
            pltpu.VMEM((blocks, 1, BLK), f32),
            pltpu.VMEM((blocks, PAIR, BLK), f32),
            pltpu.VMEM((blocks + extra, *tile), f32),
            pltpu.VMEM((far_rows, PAIR), f32),
            pltpu.VMEM((blocks, *tile), bf),
            pltpu.SemaphoreType.DMA((blocks,)),
        ],
        compiler_params=pltpu.CompilerParams(vmem_limit_bytes=ATTEND_LIMIT),
        cost_estimate=cost(
            link_count * 6 * BLK * BLK * PAIR * 2,
            (2 * extra + 4 * blocks) * tile_bytes,
            link_count * BLK * BLK,
        ),
        name="attend",
    )(own_index, own_links, near, far, all_qg)
    all_odq = lax.all_gather(odq, "head")

    far_out, piece = lax.optimization_barrier((far_out, piece))
    hot_turned = (all_pieces[:, None] == piece[None, :]).astype(bf)
    returned = lax.all_to_all(far_out, "slab", split_axis=0, concat_axis=0, tiled=True)
    summed = pl.pallas_call(
        functools.partial(reduce_kernel, **sizes),
        out_shape=jax.ShapeDtypeStruct((spread_rows, PAIR), bf),
        in_specs=[VMEM, VMEM],
        out_specs=VMEM,
        scratch_shapes=[
            pltpu.VMEM((far_rows, PAIR), f32),
            pltpu.VMEM((slabs * extra, parts * PAIR), f32),
        ],
        compiler_params=params,
        cost_estimate=cost(2 * far_rows * slabs * blocks * PAIR, 5 * blocks * tile_bytes),
        name="reduce",
    )(hot_turned, returned)
    summed = lax.all_to_all(summed, "slab", split_axis=0, concat_axis=0, tiled=True)
    dkv = pl.pallas_call(
        functools.partial(combine_kernel, slabs=slabs),
        out_shape=jax.ShapeDtypeStruct((blocks, *tile), bf),
        in_specs=[ANY, VMEM],
        out_specs=VMEM,
        scratch_shapes=[
            pltpu.VMEM((spread_rows, PAIR), f32),
            pltpu.VMEM((blocks, *tile), f32),
            pltpu.SemaphoreType.DMA,
        ],
        compiler_params=params,
        cost_estimate=cost(0, 5 * blocks * tile_bytes),
        name="combine",
    )(home, summed)
    dkv = lax.all_to_all(dkv, "head", split_axis=0, concat_axis=0, tiled=True)
    return pl.pallas_call(
        unpack_kernel,
        out_shape=tuple(jax.ShapeDtypeStruct((BLK, blocks * HD), bf) for _ in range(4)),
        in_specs=[SMEM, ANY, VMEM],
        out_specs=(ANY,) * 4,
        scratch_shapes=[
            pltpu.VMEM((blocks, *tile), bf),
            pltpu.VMEM((4, BLK, blocks * HD), bf),
            pltpu.SemaphoreType.DMA((blocks,)),
            pltpu.SemaphoreType.DMA((4,)),
        ],
        cost_estimate=cost(0, 4 * blocks * tile_bytes),
        name="unpack",
    )(own_index, all_odq, dkv)


def solution(mesh):
    rows = P(("slab", "head"), None)
    return jax.shard_map(
        body,
        mesh=mesh,
        in_specs=(rows, rows, rows, rows, P(), P()),
        out_specs=(rows,) * 4,
        check_vma=False,
    )
```

```python
import functools
import math

import jax
import jax.numpy as jnp
from jax import lax
from jax.experimental import pallas as pl
from jax.experimental.pallas import tpu as pltpu
from jax.sharding import PartitionSpec as P

HD = 64
BLK = 128
PAIR = 2 * HD
UNROLL = 8
OTHER_UNROLL = 24
FEW = 16
LIMIT = 48 * 1024 * 1024
ATTEND_LIMIT = 60 * 1024 * 1024

VMEM = pl.BlockSpec(memory_space=pltpu.VMEM)
SMEM = pl.BlockSpec(memory_space=pltpu.SMEM)
ANY = pl.BlockSpec(memory_space=pl.ANY)


def cost(flops, moved, exps=0):
    return pl.CostEstimate(flops=flops, bytes_accessed=moved, transcendentals=exps)


def most_far(links_ref, blocks):
    queried, slots = links_ref[blocks:, 0, :], links_ref[blocks:, 1, :]
    order = lax.broadcasted_iota(jnp.int32, slots.shape, 0)
    far = (queried >= 0) & (slots >= blocks)
    keys = jnp.where(far, slots, -1 - order)
    total = far[:1].astype(jnp.float32)
    for p in range(1, slots.shape[0]):
        same = (keys[:p] == keys[p : p + 1]).astype(jnp.float32)
        again = jnp.max(same, axis=0, keepdims=True)
        total = total + far[p : p + 1].astype(jnp.float32) * (1.0 - again)
    return jnp.max(total).astype(jnp.int32)


def pack_kernel(links_ref, k_ref, v_ref, q_ref, g_ref, kv_ref, qg_ref, most_ref, held, sems):
    copies = [
        pltpu.make_async_copy(ref, held.at[i], sems.at[i])
        for i, ref in enumerate((k_ref, v_ref, q_ref, g_ref))
    ]
    for copy in copies:
        copy.start()
    most_ref[0] = most_far(links_ref, kv_ref.shape[0])
    for first, out_ref in ((0, kv_ref), (2, qg_ref)):
        copies[first].wait()
        copies[first + 1].wait()
        for h in range(out_ref.shape[0]):
            cols = slice(h * HD, (h + 1) * HD)
            out_ref[h] = jnp.concatenate([held[first, :, cols], held[first + 1, :, cols]], axis=1)


def own_tiles(all_ref, index, held, sems):
    return [
        pltpu.make_async_copy(all_ref.at[i, index], held.at[i], sems.at[i])
        for i in range(held.shape[0])
    ]


def unpack_kernel(
    index_ref, odq_ref, dkv_ref, o_ref, dq_ref, dk_ref, dv_ref, held, dkv, rows, sems, dkv_sem, out_sems
):
    dkv_copy = pltpu.make_async_copy(dkv_ref, dkv, dkv_sem)
    copies = own_tiles(odq_ref, index_ref[0], held, sems)
    for copy in (dkv_copy, *copies):
        copy.start()
    outs = []
    for tiles, first, out_refs in ((dkv, 0, (dk_ref, dv_ref)), (held, 2, (dq_ref, o_ref))):
        for copy in copies if tiles is held else (dkv_copy,):
            copy.wait()
        for h in range(0, tiles.shape[0], 2):
            even, odd = tiles[h], tiles[h + 1]
            cols = slice(h * HD, (h + 2) * HD)
            rows[first, :, cols] = jnp.concatenate([even[:, :HD], odd[:, :HD]], axis=1)
            rows[first + 1, :, cols] = jnp.concatenate([even[:, HD:], odd[:, HD:]], axis=1)
        for i, out_ref in enumerate(out_refs, first):
            outs.append(pltpu.make_async_copy(rows.at[i], out_ref, out_sems.at[i]))
            outs[-1].start()
    for out in outs:
        out.wait()


def each_piece(slabs, held):
    parts = BLK // slabs
    for c in range(held):
        for part in range(parts):
            yield c, slice(part * slabs, (part + 1) * slabs), pl.ds(
                part * held + c, slabs, stride=parts * held
            )


def spread_kernel(near_ref, out_ref, wide, *, slabs):
    for c, rows, piece_rows in each_piece(slabs, near_ref.shape[0]):
        wide[piece_rows, :] = near_ref[c, rows, :].astype(jnp.float32)
    out_ref[...] = wide[...].astype(jnp.bfloat16)


def gather_kernel(hot_ref, in_ref, out_ref, wide, *, slabs, blocks, extra):
    parts = BLK // slabs
    pieces = in_ref[...].reshape(slabs, parts, blocks, PAIR)
    source = jnp.concatenate(
        [pieces[:, part].reshape(slabs * blocks, PAIR) for part in range(parts)], axis=1
    )
    for t in range(0, slabs, UNROLL):
        picked = jnp.dot(
            hot_ref[t * extra : (t + UNROLL) * extra, :],
            source,
            preferred_element_type=jnp.float32,
        )
        for r in range(UNROLL):
            for part in range(parts):
                start = ((t + r) * parts + part) * extra
                wide[start : start + extra, :] = picked[
                    r * extra : (r + 1) * extra, part * PAIR : (part + 1) * PAIR
                ]
    out_ref[...] = wide[...].astype(jnp.bfloat16)


def reduce_kernel(hot_ref, in_ref, out_ref, wide, beside, *, slabs, blocks, extra):
    parts = BLK // slabs
    wide[...] = in_ref[...].astype(jnp.float32)
    for t in range(slabs):
        for part in range(parts):
            start = (t * parts + part) * extra
            beside[t * extra : (t + 1) * extra, part * PAIR : (part + 1) * PAIR] = wide[
                start : start + extra, :
            ]
    terms = beside[...].astype(jnp.bfloat16)
    for u in range(0, slabs, UNROLL):
        summed = jnp.dot(
            hot_ref[u * blocks : (u + UNROLL) * blocks, :],
            terms,
            preferred_element_type=jnp.float32,
        ).astype(jnp.bfloat16)
        for r in range(UNROLL):
            for part in range(parts):
                start = ((u + r) * parts + part) * blocks
                out_ref[start : start + blocks, :] = summed[
                    r * blocks : (r + 1) * blocks, part * PAIR : (part + 1) * PAIR
                ]


def attend_kernel(
    index_ref,
    links_ref,
    near_ref,
    far_ref,
    all_qg_ref,
    odq_ref,
    home_ref,
    far_out_ref,
    table,
    masked,
    s_buf,
    d_buf,
    top,
    total,
    delta,
    acc,
    dkv,
    wide,
    qg,
    sems,
    near_sem,
    *,
    slabs,
):
    blocks, slots = near_ref.shape[0], table.shape[0]
    link_count = links_ref.shape[0] // 2
    copies = own_tiles(all_qg_ref, index_ref[0], qg, sems)
    copies.append(pltpu.make_async_copy(near_ref, table.at[pl.ds(0, blocks)], near_sem))
    for copy in copies:
        copy.start()
    score_scale = 1.0 / math.sqrt(HD)
    exp_scale = score_scale * math.log2(math.e)
    left = lax.broadcasted_iota(jnp.int32, (BLK, PAIR), 1) < HD

    wide[...] = far_ref[...].astype(jnp.float32)
    for p, rows, piece_rows in each_piece(slabs, slots - blocks):
        table[blocks + p, rows, :] = wide[piece_rows, :].astype(jnp.bfloat16)
    dkv[blocks:] = jnp.zeros((slots - blocks, BLK, PAIR), jnp.float32)
    for copy in copies:
        copy.wait()
    for b in range(blocks):
        own = qg[b]
        masked[b, :BLK, :] = jnp.where(left, own, jnp.zeros_like(own))
        masked[b, BLK:, :] = jnp.where(left, jnp.zeros_like(own), own)

    def each_link(step):
        def other(i, _):
            for r in range(OTHER_UNROLL):
                j = blocks + i * OTHER_UNROLL + r
                queried = links_ref[2 * j]
                step(j, jnp.maximum(queried, 0), links_ref[2 * j + 1], queried >= 0)
            return 0

        for b in range(blocks):
            step(b, b, b, None)
        lax.fori_loop(0, (link_count - blocks) // OTHER_UNROLL, other, 0)

    def score_step(j, b, s, valid):
        both = lax.dot_general(
            table[s], masked[b], (((1,), (1,)), ((), ())), preferred_element_type=jnp.float32
        )
        s_buf[j] = both[:, :BLK]
        d_buf[j] = both[:, BLK:]
        largest = jnp.max(both[:, :BLK], axis=0, keepdims=True)
        if valid is None:
            top[b] = largest
        else:
            top[b] = jnp.maximum(top[b], jnp.where(valid, largest, -3e38))

    def sum_step(j, b, s, valid):
        shift = top[b] if valid is None else top[b] + jnp.where(valid, 0.0, 1e30)
        raised = jnp.exp2((s_buf[j] - shift) * exp_scale)
        s_buf[j] = raised
        part = jnp.sum(raised, axis=0, keepdims=True)
        weighted = jnp.sum(raised * d_buf[j], axis=0, keepdims=True)
        total[b] = part if valid is None else total[b] + part
        delta[b] = weighted if valid is None else delta[b] + weighted

    def grad_step(j, b, s, valid):
        prob = (s_buf[j] * total[b]).astype(jnp.bfloat16)
        dscore = (prob.astype(jnp.float32) * (d_buf[j] - delta[b]) * score_scale).astype(
            jnp.bfloat16
        )
        turned = lax.dot_general(
            table[s],
            jnp.concatenate([prob, dscore], axis=1),
            (((0,), (0,)), ((), ())),
            preferred_element_type=jnp.float32,
        )
        terms = jnp.dot(
            jnp.concatenate([dscore, prob], axis=0),
            qg[b],
            preferred_element_type=jnp.float32,
        )
        both = jnp.where(left, terms[:BLK], terms[BLK:])
        if valid is None:
            acc[b, :HD, :] = turned[:HD, BLK:]
            acc[b, HD:, :] = turned[HD:, :BLK]
            dkv[s] = both
        else:
            acc[b, :HD, :] += turned[:HD, BLK:]
            acc[b, HD:, :] += turned[HD:, :BLK]
            dkv[s] += both

    each_link(score_step)
    each_link(sum_step)
    inverse = 1.0 / total[...]
    delta[...] = delta[...] * inverse
    total[...] = inverse
    each_link(grad_step)

    for p, rows, piece_rows in each_piece(slabs, slots - blocks):
        wide[piece_rows, :] = dkv[blocks + p, rows, :]
    far_out_ref[...] = wide[...].astype(jnp.bfloat16)
    for b in range(blocks):
        odq_ref[b] = acc[b].T.astype(jnp.bfloat16)
    home_ref[...] = dkv[:blocks]


def combine_kernel(home_ref, returned_ref, out_ref, wide, home, sem, *, slabs):
    copy = pltpu.make_async_copy(home_ref, home, sem)
    copy.start()
    wide[...] = returned_ref[...].astype(jnp.float32)
    copy.wait()
    for c, rows, piece_rows in each_piece(slabs, home.shape[0]):
        out_ref[c, rows, :] = (home[c, rows, :] + wide[piece_rows, :]).astype(jnp.bfloat16)


def body(queries, keys, values, out_grad, links, wanted):
    blocks = lax.axis_size("head")
    extra = links.shape[1] - blocks
    bf = jnp.bfloat16
    kv, qg, most = pl.pallas_call(
        pack_kernel,
        out_shape=(
            jax.ShapeDtypeStruct((blocks, BLK, PAIR), bf),
            jax.ShapeDtypeStruct((blocks, BLK, PAIR), bf),
            jax.ShapeDtypeStruct((1,), jnp.int32),
        ),
        in_specs=[VMEM] + [ANY] * 4,
        out_specs=(VMEM, VMEM, SMEM),
        scratch_shapes=[
            pltpu.VMEM((4, *queries.shape), bf),
            pltpu.SemaphoreType.DMA((4,)),
        ],
        cost_estimate=cost(0, 16 * blocks * BLK * PAIR),
        name="pack",
    )(links.transpose(1, 2, 0), keys, values, queries, out_grad)
    given = (kv, qg, links, wanted)
    if extra <= FEW:
        return step(*given, extra=extra)
    return lax.cond(
        most[0] <= FEW,
        functools.partial(step, extra=FEW),
        functools.partial(step, extra=extra),
        *given,
    )


def step(kv, qg, links, wanted, *, extra):
    slabs = lax.axis_size("slab")
    blocks = lax.axis_size("head")
    slab_index = lax.axis_index("slab")
    own_index = lax.axis_index("head").astype(jnp.int32).reshape(1)
    link_count = links.shape[1]
    parts = BLK // slabs
    bf, f32 = jnp.bfloat16, jnp.float32
    params = pltpu.CompilerParams(vmem_limit_bytes=LIMIT)
    tile = (BLK, PAIR)
    tile_bytes = 2 * BLK * PAIR
    sizes = dict(slabs=slabs, blocks=blocks, extra=extra)
    spread_rows, far_rows = slabs * parts * blocks, slabs * parts * extra

    named = links[:, blocks:, 1] - blocks
    hit = named[:, :, None] == jnp.arange(slabs, dtype=jnp.int32)
    used = jnp.any(hit & (links[:, blocks:, :1] >= 0), 1)
    slab_ids = jnp.arange(slabs, dtype=jnp.int32)
    before = (slab_ids[:, None] < slab_ids[None, :]).astype(bf)
    place = jnp.dot(used.astype(bf), before, preferred_element_type=f32).astype(jnp.int32)
    places = jnp.arange(extra, dtype=jnp.int32)
    at = used[:, None, :] & (place[:, None, :] == places[None, :, None])
    row = slab_ids[None, :] * blocks + wanted
    piece = jnp.sum(jnp.where(at, row[:, None, :] + 1, 0), -1).reshape(-1) - 1
    all_pieces = jnp.arange(slabs * blocks, dtype=jnp.int32)
    hot = (piece[:, None] == all_pieces[None, :]).astype(bf)
    own_links = lax.dynamic_index_in_dim(links, slab_index, 0, keepdims=False)
    own_place = lax.dynamic_index_in_dim(place, slab_index, 0, keepdims=False)
    own_named = own_links[:, 1] - blocks
    own_place = jnp.sum(jnp.where(own_named[:, None] == slab_ids, own_place, 0), -1)
    own_slots = jnp.where(
        own_named >= 0, blocks + jnp.minimum(own_place, extra - 1), own_links[:, 1]
    )
    own_links = jnp.stack([own_links[:, 0], own_slots], -1).reshape(-1)

    near = lax.all_to_all(kv, "head", split_axis=0, concat_axis=0, tiled=True)
    all_qg = lax.all_gather(qg, "head")

    pieces = pl.pallas_call(
        functools.partial(spread_kernel, slabs=slabs),
        out_shape=jax.ShapeDtypeStruct((spread_rows, PAIR), bf),
        in_specs=[VMEM],
        out_specs=VMEM,
        scratch_shapes=[pltpu.VMEM((spread_rows, PAIR), f32)],
        compiler_params=params,
        cost_estimate=cost(0, 2 * blocks * tile_bytes),
        name="spread",
    )(near)
    pieces = lax.all_to_all(pieces, "slab", split_axis=0, concat_axis=0, tiled=True)
    pieces, own_links = lax.optimization_barrier((pieces, own_links))
    chosen = pl.pallas_call(
        functools.partial(gather_kernel, **sizes),
        out_shape=jax.ShapeDtypeStruct((far_rows, PAIR), bf),
        in_specs=[VMEM, VMEM],
        out_specs=VMEM,
        scratch_shapes=[pltpu.VMEM((far_rows, PAIR), f32)],
        compiler_params=params,
        cost_estimate=cost(2 * far_rows * slabs * blocks * PAIR, 5 * blocks * tile_bytes),
        name="gather",
    )(hot, pieces)
    far = lax.all_to_all(chosen, "slab", split_axis=0, concat_axis=0, tiled=True)

    odq, home, far_out = pl.pallas_call(
        functools.partial(attend_kernel, slabs=slabs),
        out_shape=(
            jax.ShapeDtypeStruct((blocks, *tile), bf),
            jax.ShapeDtypeStruct((blocks, *tile), f32),
            jax.ShapeDtypeStruct((far_rows, PAIR), bf),
        ),
        in_specs=[SMEM, SMEM, ANY, VMEM, ANY],
        out_specs=(VMEM, VMEM, VMEM),
        scratch_shapes=[
            pltpu.VMEM((blocks + extra, *tile), bf),
            pltpu.VMEM((blocks, 2 * BLK, PAIR), bf),
            pltpu.VMEM((link_count, BLK, BLK), f32),
            pltpu.VMEM((link_count, BLK, BLK), f32),
            pltpu.VMEM((blocks, 1, BLK), f32),
            pltpu.VMEM((blocks, 1, BLK), f32),
            pltpu.VMEM((blocks, 1, BLK), f32),
            pltpu.VMEM((blocks, PAIR, BLK), f32),
            pltpu.VMEM((blocks + extra, *tile), f32),
            pltpu.VMEM((far_rows, PAIR), f32),
            pltpu.VMEM((blocks, *tile), bf),
            pltpu.SemaphoreType.DMA((blocks,)),
            pltpu.SemaphoreType.DMA,
        ],
        compiler_params=pltpu.CompilerParams(vmem_limit_bytes=ATTEND_LIMIT),
        cost_estimate=cost(
            link_count * 6 * BLK * BLK * PAIR * 2,
            (2 * extra + 4 * blocks) * tile_bytes,
            link_count * BLK * BLK,
        ),
        name="attend",
    )(own_index, own_links, near, far, all_qg)
    all_odq = lax.all_gather(odq, "head")

    far_out, piece = lax.optimization_barrier((far_out, piece))
    hot_turned = (all_pieces[:, None] == piece[None, :]).astype(bf)
    returned = lax.all_to_all(far_out, "slab", split_axis=0, concat_axis=0, tiled=True)
    summed = pl.pallas_call(
        functools.partial(reduce_kernel, **sizes),
        out_shape=jax.ShapeDtypeStruct((spread_rows, PAIR), bf),
        in_specs=[VMEM, VMEM],
        out_specs=VMEM,
        scratch_shapes=[
            pltpu.VMEM((far_rows, PAIR), f32),
            pltpu.VMEM((slabs * extra, parts * PAIR), f32),
        ],
        compiler_params=params,
        cost_estimate=cost(2 * far_rows * slabs * blocks * PAIR, 5 * blocks * tile_bytes),
        name="reduce",
    )(hot_turned, returned)
    summed = lax.all_to_all(summed, "slab", split_axis=0, concat_axis=0, tiled=True)
    dkv = pl.pallas_call(
        functools.partial(combine_kernel, slabs=slabs),
        out_shape=jax.ShapeDtypeStruct((blocks, *tile), bf),
        in_specs=[ANY, VMEM],
        out_specs=VMEM,
        scratch_shapes=[
            pltpu.VMEM((spread_rows, PAIR), f32),
            pltpu.VMEM((blocks, *tile), f32),
            pltpu.SemaphoreType.DMA,
        ],
        compiler_params=params,
        cost_estimate=cost(0, 5 * blocks * tile_bytes),
        name="combine",
    )(home, summed)
    dkv = lax.all_to_all(dkv, "head", split_axis=0, concat_axis=0, tiled=True)
    return pl.pallas_call(
        unpack_kernel,
        out_shape=tuple(jax.ShapeDtypeStruct((BLK, blocks * HD), bf) for _ in range(4)),
        in_specs=[SMEM, ANY, ANY],
        out_specs=(ANY,) * 4,
        scratch_shapes=[
            pltpu.VMEM((blocks, *tile), bf),
            pltpu.VMEM((blocks, *tile), bf),
            pltpu.VMEM((4, BLK, blocks * HD), bf),
            pltpu.SemaphoreType.DMA((blocks,)),
            pltpu.SemaphoreType.DMA,
            pltpu.SemaphoreType.DMA((4,)),
        ],
        cost_estimate=cost(0, 4 * blocks * tile_bytes),
        name="unpack",
    )(own_index, all_odq, dkv)


def solution(mesh):
    rows = P(("slab", "head"), None)
    return jax.shard_map(
        body,
        mesh=mesh,
        in_specs=(rows, rows, rows, rows, P(), P()),
        out_specs=(rows,) * 4,
        check_vma=False,
    )
```

```python
import functools
import math

import jax
import jax.numpy as jnp
from jax import lax
from jax.experimental import pallas as pl
from jax.experimental.pallas import tpu as pltpu
from jax.sharding import PartitionSpec as P

HD = 64
BLK = 128
PAIR = 2 * HD
UNROLL = 8
OTHER_UNROLL = 24
FEW = 16
LIMIT = 48 * 1024 * 1024
ATTEND_LIMIT = 60 * 1024 * 1024

VMEM = pl.BlockSpec(memory_space=pltpu.VMEM)
SMEM = pl.BlockSpec(memory_space=pltpu.SMEM)
ANY = pl.BlockSpec(memory_space=pl.ANY)


def cost(flops, moved, exps=0):
    return pl.CostEstimate(flops=flops, bytes_accessed=moved, transcendentals=exps)


def most_far(links_ref, blocks):
    queried, slots = links_ref[blocks:, 0, :], links_ref[blocks:, 1, :]
    order = lax.broadcasted_iota(jnp.int32, slots.shape, 0)
    far = (queried >= 0) & (slots >= blocks)
    keys = jnp.where(far, slots, -1 - order)
    total = far[:1].astype(jnp.float32)
    for p in range(1, slots.shape[0]):
        same = (keys[:p] == keys[p : p + 1]).astype(jnp.float32)
        again = jnp.max(same, axis=0, keepdims=True)
        total = total + far[p : p + 1].astype(jnp.float32) * (1.0 - again)
    return jnp.max(total).astype(jnp.int32)


def pack_kernel(
    links_ref, k_ref, v_ref, q_ref, g_ref, kv_ref, qg_ref, most_ref, held, links, sems, links_sem
):
    copies = [
        pltpu.make_async_copy(ref, held.at[i], sems.at[i])
        for i, ref in enumerate((k_ref, v_ref, q_ref, g_ref))
    ]
    links_copy = pltpu.make_async_copy(links_ref, links, links_sem)
    for copy in (*copies, links_copy):
        copy.start()
    for first, out_ref in ((0, kv_ref), (2, qg_ref)):
        copies[first].wait()
        copies[first + 1].wait()
        for h in range(out_ref.shape[0]):
            cols = slice(h * HD, (h + 1) * HD)
            out_ref[h] = jnp.concatenate([held[first, :, cols], held[first + 1, :, cols]], axis=1)
    links_copy.wait()
    most_ref[0] = most_far(links, kv_ref.shape[0])


def own_tiles(all_ref, index, held, sems):
    return [
        pltpu.make_async_copy(all_ref.at[i, index], held.at[i], sems.at[i])
        for i in range(held.shape[0])
    ]


def unpack_kernel(
    index_ref, odq_ref, dkv_ref, o_ref, dq_ref, dk_ref, dv_ref, held, dkv, rows, sems, dkv_sem, out_sems
):
    dkv_copy = pltpu.make_async_copy(dkv_ref, dkv, dkv_sem)
    copies = own_tiles(odq_ref, index_ref[0], held, sems)
    for copy in (dkv_copy, *copies):
        copy.start()
    outs = []
    for tiles, first, out_refs in ((dkv, 0, (dk_ref, dv_ref)), (held, 2, (dq_ref, o_ref))):
        for copy in copies if tiles is held else (dkv_copy,):
            copy.wait()
        for h in range(0, tiles.shape[0], 2):
            even, odd = tiles[h], tiles[h + 1]
            cols = slice(h * HD, (h + 2) * HD)
            rows[first, :, cols] = jnp.concatenate([even[:, :HD], odd[:, :HD]], axis=1)
            rows[first + 1, :, cols] = jnp.concatenate([even[:, HD:], odd[:, HD:]], axis=1)
        for i, out_ref in enumerate(out_refs, first):
            outs.append(pltpu.make_async_copy(rows.at[i], out_ref, out_sems.at[i]))
            outs[-1].start()
    for out in outs:
        out.wait()


def each_piece(slabs, held):
    parts = BLK // slabs
    for c in range(held):
        for part in range(parts):
            yield c, slice(part * slabs, (part + 1) * slabs), pl.ds(
                part * held + c, slabs, stride=parts * held
            )


def spread_kernel(near_ref, out_ref, wide, *, slabs):
    for c, rows, piece_rows in each_piece(slabs, near_ref.shape[0]):
        wide[piece_rows, :] = near_ref[c, rows, :].astype(jnp.float32)
    out_ref[...] = wide[...].astype(jnp.bfloat16)


def gather_kernel(hot_ref, in_ref, out_ref, wide, *, slabs, blocks, extra):
    parts = BLK // slabs
    pieces = in_ref[...].reshape(slabs, parts, blocks, PAIR)
    source = jnp.concatenate(
        [pieces[:, part].reshape(slabs * blocks, PAIR) for part in range(parts)], axis=1
    )
    for t in range(0, slabs, UNROLL):
        picked = jnp.dot(
            hot_ref[t * extra : (t + UNROLL) * extra, :],
            source,
            preferred_element_type=jnp.float32,
        )
        for r in range(UNROLL):
            for part in range(parts):
                start = ((t + r) * parts + part) * extra
                wide[start : start + extra, :] = picked[
                    r * extra : (r + 1) * extra, part * PAIR : (part + 1) * PAIR
                ]
    out_ref[...] = wide[...].astype(jnp.bfloat16)


def reduce_kernel(hot_ref, in_ref, out_ref, wide, beside, *, slabs, blocks, extra):
    parts = BLK // slabs
    wide[...] = in_ref[...].astype(jnp.float32)
    for t in range(slabs):
        for part in range(parts):
            start = (t * parts + part) * extra
            beside[t * extra : (t + 1) * extra, part * PAIR : (part + 1) * PAIR] = wide[
                start : start + extra, :
            ]
    terms = beside[...].astype(jnp.bfloat16)
    for u in range(0, slabs, UNROLL):
        summed = jnp.dot(
            hot_ref[u * blocks : (u + UNROLL) * blocks, :],
            terms,
            preferred_element_type=jnp.float32,
        ).astype(jnp.bfloat16)
        for r in range(UNROLL):
            for part in range(parts):
                start = ((u + r) * parts + part) * blocks
                out_ref[start : start + blocks, :] = summed[
                    r * blocks : (r + 1) * blocks, part * PAIR : (part + 1) * PAIR
                ]


def attend_kernel(
    index_ref,
    links_ref,
    near_ref,
    far_ref,
    all_qg_ref,
    odq_ref,
    home_ref,
    far_out_ref,
    table,
    masked,
    s_buf,
    d_buf,
    top,
    total,
    delta,
    acc,
    dkv,
    wide,
    qg,
    sems,
    near_sem,
    *,
    slabs,
):
    blocks, slots = near_ref.shape[0], table.shape[0]
    link_count = links_ref.shape[0] // 2
    copies = own_tiles(all_qg_ref, index_ref[0], qg, sems)
    copies.append(pltpu.make_async_copy(near_ref, table.at[pl.ds(0, blocks)], near_sem))
    for copy in copies:
        copy.start()
    score_scale = 1.0 / math.sqrt(HD)
    exp_scale = score_scale * math.log2(math.e)
    left = lax.broadcasted_iota(jnp.int32, (BLK, PAIR), 1) < HD

    wide[...] = far_ref[...].astype(jnp.float32)
    for p, rows, piece_rows in each_piece(slabs, slots - blocks):
        table[blocks + p, rows, :] = wide[piece_rows, :].astype(jnp.bfloat16)
    dkv[blocks:] = jnp.zeros((slots - blocks, BLK, PAIR), jnp.float32)
    for copy in copies:
        copy.wait()
    for b in range(blocks):
        own = qg[b]
        masked[b, :BLK, :] = jnp.where(left, own, jnp.zeros_like(own))
        masked[b, BLK:, :] = jnp.where(left, jnp.zeros_like(own), own)

    def each_link(step):
        def other(i, _):
            for r in range(OTHER_UNROLL):
                j = blocks + i * OTHER_UNROLL + r
                queried = links_ref[2 * j]
                step(j, jnp.maximum(queried, 0), links_ref[2 * j + 1], queried >= 0)
            return 0

        for b in range(blocks):
            step(b, b, b, None)
        lax.fori_loop(0, (link_count - blocks) // OTHER_UNROLL, other, 0)

    def score_step(j, b, s, valid):
        both = lax.dot_general(
            table[s], masked[b], (((1,), (1,)), ((), ())), preferred_element_type=jnp.float32
        )
        s_buf[j] = both[:, :BLK]
        d_buf[j] = both[:, BLK:]
        largest = jnp.max(both[:, :BLK], axis=0, keepdims=True)
        if valid is None:
            top[b] = largest
        else:
            top[b] = jnp.maximum(top[b], jnp.where(valid, largest, -3e38))

    def sum_step(j, b, s, valid):
        shift = top[b] if valid is None else top[b] + jnp.where(valid, 0.0, 1e30)
        raised = jnp.exp2((s_buf[j] - shift) * exp_scale)
        s_buf[j] = raised
        part = jnp.sum(raised, axis=0, keepdims=True)
        weighted = jnp.sum(raised * d_buf[j], axis=0, keepdims=True)
        total[b] = part if valid is None else total[b] + part
        delta[b] = weighted if valid is None else delta[b] + weighted

    def grad_step(j, b, s, valid):
        prob = (s_buf[j] * total[b]).astype(jnp.bfloat16)
        dscore = (prob.astype(jnp.float32) * (d_buf[j] - delta[b]) * score_scale).astype(
            jnp.bfloat16
        )
        turned = lax.dot_general(
            table[s],
            jnp.concatenate([prob, dscore], axis=1),
            (((0,), (0,)), ((), ())),
            preferred_element_type=jnp.float32,
        )
        terms = jnp.dot(
            jnp.concatenate([dscore, prob], axis=0),
            qg[b],
            preferred_element_type=jnp.float32,
        )
        both = jnp.where(left, terms[:BLK], terms[BLK:])
        if valid is None:
            acc[b, :HD, :] = turned[:HD, BLK:]
            acc[b, HD:, :] = turned[HD:, :BLK]
            dkv[s] = both
        else:
            acc[b, :HD, :] += turned[:HD, BLK:]
            acc[b, HD:, :] += turned[HD:, :BLK]
            dkv[s] += both

    each_link(score_step)
    each_link(sum_step)
    inverse = 1.0 / total[...]
    delta[...] = delta[...] * inverse
    total[...] = inverse
    each_link(grad_step)

    for p, rows, piece_rows in each_piece(slabs, slots - blocks):
        wide[piece_rows, :] = dkv[blocks + p, rows, :]
    far_out_ref[...] = wide[...].astype(jnp.bfloat16)
    for b in range(blocks):
        odq_ref[b] = acc[b].T.astype(jnp.bfloat16)
    home_ref[...] = dkv[:blocks]


def combine_kernel(home_ref, returned_ref, out_ref, wide, home, sem, *, slabs):
    copy = pltpu.make_async_copy(home_ref, home, sem)
    copy.start()
    wide[...] = returned_ref[...].astype(jnp.float32)
    copy.wait()
    for c, rows, piece_rows in each_piece(slabs, home.shape[0]):
        out_ref[c, rows, :] = (home[c, rows, :] + wide[piece_rows, :]).astype(jnp.bfloat16)


def body(queries, keys, values, out_grad, links, wanted):
    blocks = lax.axis_size("head")
    extra = links.shape[1] - blocks
    bf = jnp.bfloat16
    kv, qg, most = pl.pallas_call(
        pack_kernel,
        out_shape=(
            jax.ShapeDtypeStruct((blocks, BLK, PAIR), bf),
            jax.ShapeDtypeStruct((blocks, BLK, PAIR), bf),
            jax.ShapeDtypeStruct((1,), jnp.int32),
        ),
        in_specs=[ANY] * 5,
        out_specs=(VMEM, VMEM, SMEM),
        scratch_shapes=[
            pltpu.VMEM((4, *queries.shape), bf),
            pltpu.VMEM((links.shape[1], links.shape[2], links.shape[0]), jnp.int32),
            pltpu.SemaphoreType.DMA((4,)),
            pltpu.SemaphoreType.DMA,
        ],
        cost_estimate=cost(0, 16 * blocks * BLK * PAIR),
        name="pack",
    )(links.transpose(1, 2, 0), keys, values, queries, out_grad)
    given = (kv, qg, links, wanted)
    if extra <= FEW:
        return step(*given, extra=extra)
    return lax.cond(
        most[0] <= FEW,
        functools.partial(step, extra=FEW),
        functools.partial(step, extra=extra),
        *given,
    )


def step(kv, qg, links, wanted, *, extra):
    slabs = lax.axis_size("slab")
    blocks = lax.axis_size("head")
    slab_index = lax.axis_index("slab")
    own_index = lax.axis_index("head").astype(jnp.int32).reshape(1)
    link_count = links.shape[1]
    parts = BLK // slabs
    bf, f32 = jnp.bfloat16, jnp.float32
    params = pltpu.CompilerParams(vmem_limit_bytes=LIMIT)
    tile = (BLK, PAIR)
    tile_bytes = 2 * BLK * PAIR
    sizes = dict(slabs=slabs, blocks=blocks, extra=extra)
    spread_rows, far_rows = slabs * parts * blocks, slabs * parts * extra

    named = links[:, blocks:, 1] - blocks
    hit = named[:, :, None] == jnp.arange(slabs, dtype=jnp.int32)
    used = jnp.any(hit & (links[:, blocks:, :1] >= 0), 1)
    slab_ids = jnp.arange(slabs, dtype=jnp.int32)
    before = (slab_ids[:, None] < slab_ids[None, :]).astype(bf)
    place = jnp.dot(used.astype(bf), before, preferred_element_type=f32).astype(jnp.int32)
    places = jnp.arange(extra, dtype=jnp.int32)
    at = used[:, None, :] & (place[:, None, :] == places[None, :, None])
    row = slab_ids[None, :] * blocks + wanted
    piece = jnp.sum(jnp.where(at, row[:, None, :] + 1, 0), -1).reshape(-1) - 1
    all_pieces = jnp.arange(slabs * blocks, dtype=jnp.int32)
    hot = (piece[:, None] == all_pieces[None, :]).astype(bf)
    own_links = lax.dynamic_index_in_dim(links, slab_index, 0, keepdims=False)
    own_place = lax.dynamic_index_in_dim(place, slab_index, 0, keepdims=False)
    own_named = own_links[:, 1] - blocks
    own_place = jnp.sum(jnp.where(own_named[:, None] == slab_ids, own_place, 0), -1)
    own_slots = jnp.where(
        own_named >= 0, blocks + jnp.minimum(own_place, extra - 1), own_links[:, 1]
    )
    own_links = jnp.stack([own_links[:, 0], own_slots], -1).reshape(-1)

    near = lax.all_to_all(kv, "head", split_axis=0, concat_axis=0, tiled=True)
    all_qg = lax.all_gather(qg, "head")

    pieces = pl.pallas_call(
        functools.partial(spread_kernel, slabs=slabs),
        out_shape=jax.ShapeDtypeStruct((spread_rows, PAIR), bf),
        in_specs=[VMEM],
        out_specs=VMEM,
        scratch_shapes=[pltpu.VMEM((spread_rows, PAIR), f32)],
        compiler_params=params,
        cost_estimate=cost(0, 2 * blocks * tile_bytes),
        name="spread",
    )(near)
    pieces = lax.all_to_all(pieces, "slab", split_axis=0, concat_axis=0, tiled=True)
    pieces, own_links = lax.optimization_barrier((pieces, own_links))
    chosen = pl.pallas_call(
        functools.partial(gather_kernel, **sizes),
        out_shape=jax.ShapeDtypeStruct((far_rows, PAIR), bf),
        in_specs=[VMEM, VMEM],
        out_specs=VMEM,
        scratch_shapes=[pltpu.VMEM((far_rows, PAIR), f32)],
        compiler_params=params,
        cost_estimate=cost(2 * far_rows * slabs * blocks * PAIR, 5 * blocks * tile_bytes),
        name="gather",
    )(hot, pieces)
    far = lax.all_to_all(chosen, "slab", split_axis=0, concat_axis=0, tiled=True)

    odq, home, far_out = pl.pallas_call(
        functools.partial(attend_kernel, slabs=slabs),
        out_shape=(
            jax.ShapeDtypeStruct((blocks, *tile), bf),
            jax.ShapeDtypeStruct((blocks, *tile), f32),
            jax.ShapeDtypeStruct((far_rows, PAIR), bf),
        ),
        in_specs=[SMEM, SMEM, ANY, VMEM, ANY],
        out_specs=(VMEM, VMEM, VMEM),
        scratch_shapes=[
            pltpu.VMEM((blocks + extra, *tile), bf),
            pltpu.VMEM((blocks, 2 * BLK, PAIR), bf),
            pltpu.VMEM((link_count, BLK, BLK), f32),
            pltpu.VMEM((link_count, BLK, BLK), f32),
            pltpu.VMEM((blocks, 1, BLK), f32),
            pltpu.VMEM((blocks, 1, BLK), f32),
            pltpu.VMEM((blocks, 1, BLK), f32),
            pltpu.VMEM((blocks, PAIR, BLK), f32),
            pltpu.VMEM((blocks + extra, *tile), f32),
            pltpu.VMEM((far_rows, PAIR), f32),
            pltpu.VMEM((blocks, *tile), bf),
            pltpu.SemaphoreType.DMA((blocks,)),
            pltpu.SemaphoreType.DMA,
        ],
        compiler_params=pltpu.CompilerParams(vmem_limit_bytes=ATTEND_LIMIT),
        cost_estimate=cost(
            link_count * 6 * BLK * BLK * PAIR * 2,
            (2 * extra + 4 * blocks) * tile_bytes,
            link_count * BLK * BLK,
        ),
        name="attend",
    )(own_index, own_links, near, far, all_qg)
    all_odq = lax.all_gather(odq, "head")

    far_out, piece = lax.optimization_barrier((far_out, piece))
    hot_turned = (all_pieces[:, None] == piece[None, :]).astype(bf)
    returned = lax.all_to_all(far_out, "slab", split_axis=0, concat_axis=0, tiled=True)
    summed = pl.pallas_call(
        functools.partial(reduce_kernel, **sizes),
        out_shape=jax.ShapeDtypeStruct((spread_rows, PAIR), bf),
        in_specs=[VMEM, VMEM],
        out_specs=VMEM,
        scratch_shapes=[
            pltpu.VMEM((far_rows, PAIR), f32),
            pltpu.VMEM((slabs * extra, parts * PAIR), f32),
        ],
        compiler_params=params,
        cost_estimate=cost(2 * far_rows * slabs * blocks * PAIR, 5 * blocks * tile_bytes),
        name="reduce",
    )(hot_turned, returned)
    summed = lax.all_to_all(summed, "slab", split_axis=0, concat_axis=0, tiled=True)
    dkv = pl.pallas_call(
        functools.partial(combine_kernel, slabs=slabs),
        out_shape=jax.ShapeDtypeStruct((blocks, *tile), bf),
        in_specs=[ANY, VMEM],
        out_specs=VMEM,
        scratch_shapes=[
            pltpu.VMEM((spread_rows, PAIR), f32),
            pltpu.VMEM((blocks, *tile), f32),
            pltpu.SemaphoreType.DMA,
        ],
        compiler_params=params,
        cost_estimate=cost(0, 5 * blocks * tile_bytes),
        name="combine",
    )(home, summed)
    dkv = lax.all_to_all(dkv, "head", split_axis=0, concat_axis=0, tiled=True)
    return pl.pallas_call(
        unpack_kernel,
        out_shape=tuple(jax.ShapeDtypeStruct((BLK, blocks * HD), bf) for _ in range(4)),
        in_specs=[SMEM, ANY, ANY],
        out_specs=(ANY,) * 4,
        scratch_shapes=[
            pltpu.VMEM((blocks, *tile), bf),
            pltpu.VMEM((blocks, *tile), bf),
            pltpu.VMEM((4, BLK, blocks * HD), bf),
            pltpu.SemaphoreType.DMA((blocks,)),
            pltpu.SemaphoreType.DMA,
            pltpu.SemaphoreType.DMA((4,)),
        ],
        cost_estimate=cost(0, 4 * blocks * tile_bytes),
        name="unpack",
    )(own_index, all_odq, dkv)


def solution(mesh):
    rows = P(("slab", "head"), None)
    return jax.shard_map(
        body,
        mesh=mesh,
        in_specs=(rows, rows, rows, rows, P(), P()),
        out_specs=(rows,) * 4,
        check_vma=False,
    )
```
